32 devices in a mesh: gx: 4 (over y, core), gy: 8 (over z, x).
Axes of the slice: x: 2, y: 2, z: 4, core: 2. Of those that a mesh axis runs over, the one named last changes fastest.
Arguments:
- right_side: float32 [64, 256, 256], P('gx', 'gy'), may hold values from -30 to 30
- start_field: float32 [64, 256, 256], P('gx', 'gy'), may hold values from -1.8 to 1.8
- coef: float32 [64, 256, 256], P('gx', 'gy'), may hold values from 0.5 to 2
- deflation: float32 [8, 64, 256, 256], P(None, 'gx', 'gy'), may hold values from -9 to 9
Outputs:
- solution: float32 [64, 256, 256], P('gx', 'gy')
- residual: float32 [64, 256, 256], P('gx', 'gy')
- direction: float32 [64, 256, 256], P('gx', 'gy')
The draws below stay inside these ranges and needn't reach their ends.
All inputs are finite; a program needn't handle non-finite values.
Results may differ from the reference program's by a relative error of at most 0.0003.
Values sent between devices are 32-bit elements; how exact they have to be, the bound alone decides.
No kernel may reach another device: no remote copies, remote signals or barrier semaphores. Data moves between devices by JAX's collectives and lax.ppermute only.
A program may use at most 192 MiB of HBM per device.

```python
import math
import jax
import jax.numpy as jnp
from jax import lax

CX = 16
CY = 32
NZ = 256
K = 8
ITERS = 2
NX = 64
NY = 256
N_GX = 4
N_GY = 8


def mode_tables():
    local_rows = (jnp.arange(NX) % CX).astype(jnp.float32)
    local_cols = (jnp.arange(NY) % CY).astype(jnp.float32)
    depth = jnp.arange(NZ).astype(jnp.float32)
    pattern = jnp.arange(8)
    freq_rows = (pattern % 2).astype(jnp.float32)
    freq_cols = (pattern // 2 % 2).astype(jnp.float32)
    freq_depth = (pattern // 4).astype(jnp.float32)
    wave_rows = jnp.cos(math.pi * freq_rows[:, None] * (local_rows[None] + 0.5) / CX)
    wave_cols = jnp.cos(math.pi * freq_cols[:, None] * (local_cols[None] + 0.5) / CY)
    wave_depth = jnp.cos(math.pi * freq_depth[:, None] * (depth[None] + 0.5) / NZ)
    return (wave_rows[:, :, None] * wave_cols[:, None, :], wave_depth)


def draw_right_side(key, part):
    key_noise = jax.random.fold_in(key, 11)
    key_amps = jax.random.fold_in(key, 12)
    plane_modes, depth_modes = mode_tables()
    amounts = 0.5 * jax.random.truncated_normal(key_amps, -2.0, 2.0, (NX // CX, NY // CY, 8), jnp.float32)
    cell_amounts = jnp.repeat(jnp.repeat(amounts, CX, axis=0), CY, axis=1)
    smooth = jnp.einsum('xym,mxy,mz->xyz', cell_amounts, plane_modes, depth_modes)
    row_frac = (jnp.arange(NX).astype(jnp.float32) + 0.5) / NX
    col_frac = (jnp.arange(NY).astype(jnp.float32) + 0.5) / NY
    ramp = (0.5 + row_frac)[:, None, None] * (0.5 + col_frac)[None, :, None]
    hump = jnp.sin(math.pi * row_frac)[:, None, None] * jnp.sin(math.pi * col_frac)[None, :, None]
    noise = jax.random.truncated_normal(key_noise, -4.0, 4.0, (NX, NY, NZ), jnp.float32)
    noise = noise + 0.8 * hump
    return ramp * (noise + smooth)


def draw_deflation(key, part):
    key_noise = jax.random.fold_in(key, 21)
    key_mix = jax.random.fold_in(key, 22)
    plane_modes, depth_modes = mode_tables()
    mixing = jnp.eye(K, 8, dtype=jnp.float32)[None, None] + 0.4 * jax.random.truncated_normal(key_mix, -2.0, 2.0, (NX // CX, NY // CY, K, 8), jnp.float32)
    cell_mixing = jnp.repeat(jnp.repeat(mixing, CX, axis=0), CY, axis=1)
    smooth = jnp.einsum('xykm,mxy,mz->kxyz', cell_mixing, plane_modes, depth_modes)
    noise = 0.03 * jax.random.truncated_normal(key_noise, -4.0, 4.0, (K, NX, NY, NZ), jnp.float32)
    return smooth + noise


def shard_levels(own_key, dims, shards, smallest, top_value):
    loudness, own = 1.0, jax.random.fold_in(own_key, 6)
    for dim, parts in shards:
        draws = jnp.exp(jax.random.uniform(jax.random.fold_in(own, dim), (parts,), jnp.float32, smallest / len(shards), top_value / len(shards)))
        loudness = loudness * jnp.repeat(draws, dims[dim] // parts).reshape([-1 if axis == dim else 1 for axis in range(len(dims))])
    return loudness


def normal_values(stream_key, shape, deviation, reach, split=(), held_as=jnp.bfloat16):
    drawn = jax.random.normal(stream_key, shape, jnp.float32) * deviation
    if len(split) > 0:
        drawn = shard_levels(stream_key, shape, split, -0.22, 0.18) * drawn
    return jnp.clip(drawn, min=-reach, max=reach).astype(held_as)


def setup_inputs(seed: int = 0) -> dict:
    streams_of = jax.random.split(jax.random.key(seed), 5)
    right_side = draw_right_side(jax.random.fold_in(streams_of[4], 71), 0)
    start_field = normal_values(streams_of[1], (NX, NY, NZ), 0.3, 1.8, ((0, 4), (1, 8)), jnp.float32)
    coef = jnp.clip(jnp.exp(math.log(2.0) - 1.3862944 * jax.random.uniform(streams_of[2], (NX, NY, NZ), jnp.float32) ** shard_levels(streams_of[2], (NX, NY, NZ), ((0, 4), (1, 8)), -0.2, 0.2)), 0.5, 2.0)
    deflation = draw_deflation(jax.random.fold_in(streams_of[4], 71), 0)
    return {"right_side": right_side, "start_field": start_field, "coef": coef, "deflation": deflation}


highest = lax.Precision.HIGHEST

def face_coef(padded, along):
    length = padded.shape[along]
    lower_side = lax.slice_in_dim(padded, 0, length - 1, axis=along)
    upper_side = lax.slice_in_dim(padded, 1, length, axis=along)
    inside = (lower_side > 0.0) & (upper_side > 0.0)
    summed = lower_side + upper_side
    return jnp.where(inside, 2.0 * lower_side * upper_side / summed, summed)

def coefficients(coef):
    padded = jnp.pad(coef, 1)
    face_rows = face_coef(padded[:, 1:-1, 1:-1], 0)
    face_cols = face_coef(padded[1:-1, :, 1:-1], 1)
    face_depth = face_coef(padded[1:-1, 1:-1, :], 2)
    diagonal = face_rows[1:] + face_rows[:-1] + face_cols[:, 1:] + face_cols[:, :-1]
    diagonal = diagonal + face_depth[:, :, 1:] + face_depth[:, :, :-1]
    return (face_rows, face_cols, face_depth, diagonal)

def operate(values, stencil):
    face_rows, face_cols, face_depth, diagonal = stencil
    padded = jnp.pad(values, 1)
    beside = face_rows[1:] * padded[2:, 1:-1, 1:-1] + face_rows[:-1] * padded[:-2, 1:-1, 1:-1]
    beside = beside + face_cols[:, 1:] * padded[1:-1, 2:, 1:-1] + face_cols[:, :-1] * padded[1:-1, :-2, 1:-1]
    beside = beside + face_depth[:, :, 1:] * padded[1:-1, 1:-1, 2:] + face_depth[:, :, :-1] * padded[1:-1, 1:-1, :-2]
    return diagonal * values - beside

def block_operate(vectors, face_rows, face_cols, face_depth, diagonal):
    padded = jnp.pad(vectors, ((0, 0), (1, 1), (1, 1), (1, 1)))
    beside = face_rows[1:] * padded[:, 2:, 1:-1, 1:-1] + face_rows[:-1] * padded[:, :-2, 1:-1, 1:-1]
    beside = beside + face_cols[:, 1:] * padded[:, 1:-1, 2:, 1:-1] + face_cols[:, :-1] * padded[:, 1:-1, :-2, 1:-1]
    beside = beside + face_depth[:, :, 1:] * padded[:, 1:-1, 1:-1, 2:] + face_depth[:, :, :-1] * padded[:, 1:-1, 1:-1, :-2]
    return diagonal * vectors - beside

def diagonal_blocks(deflation, stencil):
    face_rows, face_cols, face_depth, diagonal = stencil

    def per_block(position):
        row_start = position // N_GY * CX
        col_start = position % N_GY * CY
        anchor = jnp.zeros((), jnp.int32)
        sub_block = lax.dynamic_slice(deflation, (anchor, row_start, col_start, anchor), (K, CX, CY, NZ))
        rows_part = lax.dynamic_slice(face_rows, (row_start, col_start, anchor), (CX + 1, CY, NZ))
        cols_part = lax.dynamic_slice(face_cols, (row_start, col_start, anchor), (CX, CY + 1, NZ))
        depth_part = lax.dynamic_slice(face_depth, (row_start, col_start, anchor), (CX, CY, NZ + 1))
        diag_part = lax.dynamic_slice(diagonal, (row_start, col_start, anchor), (CX, CY, NZ))
        acted_on = block_operate(sub_block, rows_part, cols_part, depth_part, diag_part)
        return jnp.einsum('kxyz,lxyz->kl', sub_block, acted_on, precision=highest)
    return lax.map(per_block, jnp.arange(N_GX * N_GY, dtype=jnp.int32))

def lower_blocks(deflation, stencil):
    face_rows, face_cols = (stencil[0], stencil[1])
    top_rows = deflation[:, CX - 1::CX]
    bottom_rows = deflation[:, 0::CX]
    shifted_rows = jnp.concatenate([jnp.zeros_like(top_rows[:, :1]), top_rows[:, :-1]], axis=1)
    weighted_rows = bottom_rows * face_rows[0:NX:CX][None]
    weighted_rows = weighted_rows.reshape(K, N_GX, N_GY, CY, NZ)
    shifted_rows = shifted_rows.reshape(K, N_GX, N_GY, CY, NZ)
    below_rows = -jnp.einsum('kabcz,labcz->abkl', weighted_rows, shifted_rows, precision=highest)
    top_cols = deflation[:, :, CY - 1::CY]
    bottom_cols = deflation[:, :, 0::CY]
    shifted_cols = jnp.concatenate([jnp.zeros_like(top_cols[:, :, :1]), top_cols[:, :, :-1]], axis=2)
    weighted_cols = bottom_cols * face_cols[:, 0:NY:CY][None]
    weighted_cols = weighted_cols.reshape(K, N_GX, CX, N_GY, NZ)
    shifted_cols = shifted_cols.reshape(K, N_GX, CX, N_GY, NZ)
    below_cols = -jnp.einsum('kacbz,lacbz->abkl', weighted_cols, shifted_cols, precision=highest)
    return (below_rows.reshape(N_GX * N_GY, K, K), below_cols.reshape(N_GX * N_GY, K, K))

def place(selector, blocks):
    return selector.astype(jnp.float32)[:, None, :, None] * blocks[:, :, None, :]

def place_mirror(selector, blocks):
    return selector.astype(jnp.float32)[:, None, :, None] * jnp.transpose(blocks, (2, 0, 1))[None]

def block_masks(block_count, across):
    positions = jnp.arange(block_count, dtype=jnp.int32)
    row_ids = positions[:, None]
    col_ids = positions[None, :]
    self_mask = row_ids == col_ids
    below_rows = col_ids == row_ids - across
    below_cols = (col_ids == row_ids - 1) & (row_ids % across != 0)
    above_rows = col_ids == row_ids + across
    above_cols = (col_ids == row_ids + 1) & (col_ids % across != 0)
    return (self_mask, below_rows, below_cols, above_rows, above_cols)

def restrict(deflation, values):

    def per_vector(vector):
        return (vector * values).reshape(N_GX, CX, N_GY, CY, NZ).sum(axis=(1, 3, 4))
    sums = lax.map(per_vector, deflation)
    return jnp.transpose(sums, (1, 2, 0)).reshape(-1)

def prolong(deflation, coarse_values):
    grid = jnp.transpose(coarse_values.reshape(N_GX, N_GY, K), (2, 0, 1))

    def add_one(carry, pair):
        vector, amounts = pair
        spread = vector.reshape(N_GX, CX, N_GY, CY, NZ) * amounts[:, None, :, None, None]
        return (carry + spread.reshape(NX, NY, NZ), None)
    summed, ignored = lax.scan(add_one, jnp.zeros((NX, NY, NZ), jnp.float32), (deflation, grid))
    return summed

def reference(right_side, start_field, coef, deflation):
    stencil = coefficients(coef)
    diagonal = stencil[3]
    diag_blocks = diagonal_blocks(deflation, stencil)
    below_rows, below_cols = lower_blocks(deflation, stencil)
    block_count = N_GX * N_GY
    self_mask, mask_below_rows, mask_below_cols, mask_above_rows, mask_above_cols = block_masks(block_count, N_GY)
    matrix = place(self_mask, diag_blocks) + place(mask_below_rows, below_rows) + place(mask_below_cols, below_cols)
    matrix = matrix + place_mirror(mask_above_rows, below_rows) + place_mirror(mask_above_cols, below_cols)
    matrix = matrix.reshape(block_count * K, block_count * K)
    factor = jnp.linalg.cholesky(matrix)

    def coarse(values):
        solved = jax.scipy.linalg.cho_solve((factor, True), restrict(deflation, values))
        return prolong(deflation, solved)
    solution = start_field + coarse(right_side - operate(start_field, stencil))
    residual = right_side - operate(solution, stencil)
    precond = residual / diagonal
    inner_now = jnp.sum(residual * precond)
    direction = precond - coarse(operate(precond, stencil))
    for iteration in range(ITERS):
        applied = operate(direction, stencil)
        step_size = inner_now / jnp.sum(direction * applied)
        solution = solution + step_size * direction
        residual = residual - step_size * applied
        precond = residual / diagonal
        inner_next = jnp.sum(residual * precond)
        direction = precond + inner_next / inner_now * direction - coarse(operate(precond, stencil))
        inner_now = inner_next
    return (solution, residual, direction)
```

```python
import jax
import jax.numpy as jnp
from jax import lax
from jax.sharding import PartitionSpec as P

ITERS = 2
BOTH = ("gx", "gy")
highest = lax.Precision.HIGHEST


def swap(value, axis, parity):
    count = lax.axis_size(axis)
    pairs = []
    for low in range(parity, count - 1, 2):
        pairs += [(low, low + 1), (low + 1, low)]
    return lax.ppermute(value, axis, pairs)


def halo(low, high, axis):
    even = lax.axis_index(axis) % 2 == 0
    first = swap(jnp.where(even, high, low), axis, 0)
    second = swap(jnp.where(even, low, high), axis, 1)
    return jnp.where(even, second, first), jnp.where(even, first, second)


def everywhere(payload):
    count = lax.axis_size("gx") * lax.axis_size("gy")
    return lax.all_to_all(jnp.broadcast_to(payload[None], (count,) + payload.shape), BOTH, 0, 0)


def face(lower, upper):
    summed = lower + upper
    inside = (lower > 0.0) & (upper > 0.0)
    return jnp.where(inside, 2.0 * lower * upper / summed, summed)


def row_sums(left, right):
    return jnp.einsum("kab,lab->kl", left, right, precision=highest)


def per_device(right_side, start_field, coef, deflation):
    num = deflation.shape[0]
    down, across = lax.axis_size("gx"), lax.axis_size("gy")
    blocks = down * across
    own = lax.axis_index("gx") * across + lax.axis_index("gy")

    pack_x = lambda i: jnp.concatenate([coef[i][None], start_field[i][None], deflation[:, i]])
    pack_y = lambda j: jnp.concatenate([coef[:, j][None], start_field[:, j][None], deflation[:, :, j]])
    x_low, x_high = halo(pack_x(0), pack_x(-1), "gx")
    y_low, y_high = halo(pack_y(0), pack_y(-1), "gy")

    def extend(cells, sides):
        xl, xh, yl, yh = sides
        xs = jnp.concatenate([xl[None], cells, xh[None]], 0)
        ys = jnp.concatenate([yl[:, None], cells, yh[:, None]], 1)
        zs = jnp.pad(cells, ((0, 0), (0, 0), (1, 1)))
        return xs, ys, zs

    cx, cy, cz = extend(coef, (x_low[0], x_high[0], y_low[0], y_high[0]))
    fx, fy, fz = face(cx[:-1], cx[1:]), face(cy[:, :-1], cy[:, 1:]), face(cz[:, :, :-1], cz[:, :, 1:])
    diagonal = fx[1:] + fx[:-1] + fy[:, 1:] + fy[:, :-1] + fz[:, :, 1:] + fz[:, :, :-1]

    def operate(cells, sides):
        vx, vy, vz = extend(cells, sides)
        beside = fx[1:] * vx[2:] + fx[:-1] * vx[:-2] + fy[:, 1:] * vy[:, 2:] + fy[:, :-1] * vy[:, :-2]
        beside = beside + fz[:, :, 1:] * vz[:, :, 2:] + fz[:, :, :-1] * vz[:, :, :-2]
        return diagonal * cells - beside

    none = (jnp.zeros_like(coef[0]),) * 2 + (jnp.zeros_like(coef[:, 0]),) * 2
    acted = jax.vmap(lambda v: operate(v, none))(deflation)
    diag_block = jnp.einsum("kxyz,lxyz->kl", deflation, acted, precision=highest)
    below_x = -row_sums(deflation[:, 0] * fx[0], x_low[2:])
    below_y = -row_sums(deflation[:, :, 0] * fy[:, 0], y_low[2:])
    start_residual = right_side - operate(start_field, (x_low[1], x_high[1], y_low[1], y_high[1]))

    def restrict(values):
        return jnp.einsum("kxyz,xyz->k", deflation, values, precision=highest)

    def pad_row(parts):
        flat = jnp.concatenate([p.reshape(-1) for p in parts])
        size = -(-flat.size // 128) * 128
        return jnp.pad(flat, (0, size - flat.size)).reshape(-1, 128)

    got = everywhere(pad_row([diag_block, below_x, below_y, restrict(start_residual)])).reshape(blocks, -1)
    square = num * num
    d_blocks, r_blocks, c_blocks = (got[:, i * square : (i + 1) * square].reshape(blocks, num, num) for i in range(3))
    ids = jnp.arange(blocks)
    place = lambda mask, part: jnp.where(mask[:, None, :, None], part[:, :, None, :], 0.0)
    mirror = lambda mask, part: jnp.where(mask[:, None, :, None], jnp.transpose(part, (2, 0, 1))[None], 0.0)
    rows, cols = ids[:, None], ids[None]
    matrix = place(rows == cols, d_blocks) + place(cols == rows - across, r_blocks)
    matrix = matrix + place((cols == rows - 1) & (rows % across != 0), c_blocks)
    matrix = matrix + mirror(cols == rows + across, r_blocks)
    matrix = matrix + mirror((cols == rows + 1) & (cols % across != 0), c_blocks)
    factor = jnp.linalg.cholesky(matrix.reshape(blocks * num, blocks * num))

    def solve(vector):
        solved = jax.scipy.linalg.cho_solve((factor, True), vector)
        grid = jnp.pad(solved.reshape(down, across, num), ((1, 1), (1, 1), (0, 0)))
        at = lambda i, j: lax.dynamic_slice(grid, (lax.axis_index("gx") + i, lax.axis_index("gy") + j, 0), (1, 1, num))[0, 0]
        return at(1, 1), (at(0, 1), at(2, 1), at(1, 0), at(1, 2))

    def spread(amounts):
        mine, around = amounts
        cells = jnp.einsum("kxyz,k->xyz", deflation, mine, precision=highest)
        layers = (x_low[2:], x_high[2:], y_low[2:], y_high[2:])
        sides = tuple(jnp.einsum("kab,k->ab", l, y, precision=highest) for l, y in zip(layers, around))
        return cells, operate(cells, sides)

    def full(cells):
        xl, xh = halo(cells[0], cells[-1], "gx")
        yl, yh = halo(cells[:, 0], cells[:, -1], "gy")
        return operate(cells, (xl, xh, yl, yh))

    coarse, image = spread(solve(got[:, 3 * square : 3 * square + num].reshape(-1)))
    solution = start_field + coarse
    residual = start_residual - image
    direction = applied = jnp.zeros_like(solution)
    inner = energy = jnp.float32(1.0)
    for iteration in range(ITERS + 1):
        precond = residual / diagonal
        acted_p = full(precond)
        sums = jnp.stack([jnp.sum(residual * precond), jnp.sum(precond * acted_p), jnp.sum(precond * applied)])
        got = everywhere(pad_row([sums, restrict(acted_p)]))[:, 0]
        new, energy_p, cross = (jnp.sum(got[:, i]) for i in range(3))
        vector = got[:, 3 : 3 + num].reshape(-1)
        solved = jax.scipy.linalg.cho_solve((factor, True), vector)
        grid = jnp.pad(solved.reshape(down, across, num), ((1, 1), (1, 1), (0, 0)))
        at = lambda i, j: lax.dynamic_slice(grid, (lax.axis_index("gx") + i, lax.axis_index("gy") + j, 0), (1, 1, num))[0, 0]
        coarse, image = spread((at(1, 1), (at(0, 1), at(2, 1), at(1, 0), at(1, 2))))
        beta = jnp.where(iteration == 0, 0.0, new / inner)
        direction = precond - coarse + beta * direction
        if iteration == ITERS:
            break
        applied = acted_p - image + beta * applied
        energy = energy_p - jnp.sum(solved * vector) + 2.0 * beta * cross + beta * beta * energy
        step = new / energy
        solution = solution + step * direction
        residual = residual - step * applied
        inner = new
    return solution, residual, direction


def solution(mesh):
    field = P("gx", "gy", None)
    return jax.shard_map(
        per_device,
        mesh=mesh,
        in_specs=(field, field, field, P(None, "gx", "gy", None)),
        out_specs=(field, field, field),
        check_vma=False,
    )
```

```python
import functools

import jax
import jax.numpy as jnp
from jax import lax
from jax.experimental import pallas as pl
from jax.experimental.pallas import tpu as pltpu
from jax.sharding import PartitionSpec as P

ITERS = 2
BOTH = ("gx", "gy")
HIGH = lax.Precision.HIGHEST
F32 = jnp.float32
VMEM = pl.BlockSpec(memory_space=pltpu.VMEM)
SMEM = pl.BlockSpec(memory_space=pltpu.SMEM)


def swap(value, axis, parity):
    count = lax.axis_size(axis)
    pairs = []
    for low in range(parity, count - 1, 2):
        pairs += [(low, low + 1), (low + 1, low)]
    return lax.ppermute(value, axis, pairs)


def swaps(layers):
    return [swap(v, axis, parity) for v, (axis, parity) in zip(layers, (("gx", 0), ("gx", 1), ("gy", 0), ("gy", 1)))]


def everywhere(payload):
    return lax.all_to_all(payload, BOTH, 0, 0)


def face(lower, upper):
    summed = lower + upper
    inside = (lower > 0.0) & (upper > 0.0)
    return jnp.where(inside, 2.0 * lower * upper / summed, summed)


def iota(shape, dim):
    return lax.broadcasted_iota(jnp.int32, shape, dim)


def dot(a, b):
    return lax.dot_general(a, b, (((1,), (0,)), ((), ())), precision=HIGH, preferred_element_type=F32)


def fold(x):
    pieces = [x[r : r + 8, c : c + 128] for r in range(0, x.shape[0], 8) for c in range(0, x.shape[1], 128)]
    return functools.reduce(jnp.add, pieces)


def row_of(acc, count, width):
    total = functools.reduce(jnp.add, [acc[pl.ds(s, count, stride=8), :] for s in range(8)])
    if width > count:
        total = jnp.concatenate([total, jnp.zeros((width - count, 128), F32)], 0)
    sums = lax.dot_general(jnp.ones((8, 128), F32), total, (((1,), (1,)), ((), ())), precision=HIGH, preferred_element_type=F32)
    return sums[0:1]


def add_to(acc, index, x):
    acc[pl.ds(index * 8, 8), :] += fold(x)


def beside_y(v, low, high):
    rows = v.shape[0]
    row = iota(v.shape, 0)
    below = jnp.where(row == 0, low, pltpu.roll(v, 1, 0))
    above = jnp.where(row == rows - 1, high, pltpu.roll(v, rows - 1, 0))
    return below, above


def beside_z(v):
    return pltpu.roll(v, 1, 1), pltpu.roll(v, v.shape[1] - 1, 1)


def act(i, v, before, after, low, high, faces):
    fx, fyl, fyu, fzl, fzu, diag = faces
    below, above = beside_y(v, low, high)
    left, right = beside_z(v)
    out = diag[i] * v - fx[i] * before - fx[i + 1] * after
    return out - fyl[i] * below - fyu[i] * above - fzl[i] * left - fzu[i] * right


def prepare_kernel(ids, b, x0, coef, z, rx0, rx1, ry0, ry1, fx, fyl, fyu, fzl, fzu, diag, dinv, r0, zxl, zxh, zyl, zyh, out, cext, xext, yrow, acc, zy0):
    num, nx, ny, nz = z.shape
    evx, evy = ids[0] == 1, ids[1] == 1
    cext[0] = jnp.where(evx, rx1[0], rx0[0])
    cext[nx + 1] = jnp.where(evx, rx0[0], rx1[0])
    xext[0] = jnp.where(evx, rx1[1], rx0[1])
    xext[nx + 1] = jnp.where(evx, rx0[1], rx1[1])
    for k in range(num):
        zxl[k] = jnp.where(evx, rx1[2 + k], rx0[2 + k])
        zxh[k] = jnp.where(evx, rx0[2 + k], rx1[2 + k])
        zyl[k] = jnp.where(evy, ry1[2 + k], ry0[2 + k])
        zyh[k] = jnp.where(evy, ry0[2 + k], ry1[2 + k])
    for f in range(2):
        yrow[2 * f] = jnp.where(evy, ry1[f], ry0[f])
        yrow[2 * f + 1] = jnp.where(evy, ry0[f], ry1[f])
    acc[...] = jnp.zeros_like(acc)

    def fill(i, carry):
        cext[i + 1] = coef[i]
        xext[i + 1] = x0[i]
        return carry

    lax.fori_loop(0, nx, fill, 0)

    def faces_x(i, carry):
        fx[i] = face(cext[i], cext[i + 1])
        return carry

    lax.fori_loop(0, nx + 1, faces_x, 0)
    lane, row = iota((ny, nz), 1), iota((ny, nz), 0)

    def faces_yz(i, carry):
        c = cext[i + 1]
        below, above = beside_y(c, yrow[0, pl.ds(i, 1), :], yrow[1, pl.ds(i, 1), :])
        left, right = beside_z(c)
        yl, yu = face(below, c), face(c, above)
        zl, zu = face(jnp.where(lane == 0, 0.0, left), c), face(c, jnp.where(lane == nz - 1, 0.0, right))
        d = fx[i + 1] + fx[i] + yu + yl + zu + zl
        fyl[i], fyu[i] = yl, yu
        fzl[i], fzu[i] = jnp.where(lane == 0, 0.0, zl), jnp.where(lane == nz - 1, 0.0, zu)
        diag[i] = d
        dinv[i] = 1.0 / d
        return carry

    lax.fori_loop(0, nx, faces_yz, 0)
    faces = (fx, fyl, fyu, fzl, fzu, diag)
    square = num * num

    def plane(i, carry):
        r = b[i] - act(i, xext[i + 1], xext[i], xext[i + 2], yrow[2, pl.ds(i, 1), :], yrow[3, pl.ds(i, 1), :], faces)
        r0[i] = r
        fa = jnp.where(i > 0, fx[i], 0.0)
        fb = jnp.where(i < nx - 1, fx[i + 1], 0.0)
        before, after = jnp.maximum(i - 1, 0), jnp.minimum(i + 1, nx - 1)
        yl, yu = jnp.where(row == 0, 0.0, fyl[i]), jnp.where(row == ny - 1, 0.0, fyu[i])
        for k in range(num):
            v = z[k, i]
            left, right = beside_z(v)
            w = diag[i] * v - fa * z[k, before] - fb * z[k, after] - fzl[i] * left - fzu[i] * right
            w = w - yl * pltpu.roll(v, 1, 0) - yu * pltpu.roll(v, ny - 1, 0)
            for m in range(k + 1):
                add_to(acc, 2 * square + m * num + k, w * z[m, i])
            add_to(acc, 3 * square + k, v * r)
            zy0[k, pl.ds(i, 1), :] = v[0:1, :] * fyl[i, 0:1, :]
        return carry

    lax.fori_loop(0, nx, plane, 0)
    for k in range(num):
        for m in range(k):
            acc[pl.ds((2 * square + k * num + m) * 8, 8), :] = acc[pl.ds((2 * square + m * num + k) * 8, 8), :]

    def below_blocks(k, carry):
        weighted = z[k, 0] * fx[0]
        for m in range(num):
            add_to(acc, k * num + m, weighted * zxl[m])
            add_to(acc, square + k * num + m, zy0[k] * zyl[m])
        return carry

    lax.fori_loop(0, num, below_blocks, 0)
    count = acc.shape[0] // 8
    line = row_of(acc, count, count)
    for part in range(count // 128):
        out[:, part, :] = jnp.broadcast_to(line[:, part * 128 : (part + 1) * 128], (out.shape[0], 128))


def small_inverse(p):
    size = p.shape[0]
    lane, row = iota(p.shape, 1), iota(p.shape, 0)
    head = iota((1, size), 1)
    for k in range(0, size, 2):
        r0, r1 = p[k : k + 1, :], p[k + 1 : k + 2, :]
        c0, c1 = p[:, k : k + 1], p[:, k + 1 : k + 2]
        a, b = p[k : k + 1, k : k + 1], p[k : k + 1, k + 1 : k + 2]
        c, d = p[k + 1 : k + 2, k : k + 1], p[k + 1 : k + 2, k + 1 : k + 2]
        over = 1.0 / (a * d - b * c)
        r0 = jnp.where(head == k, 1.0, jnp.where(head == k + 1, 0.0, r0))
        r1 = jnp.where(head == k, 0.0, jnp.where(head == k + 1, 1.0, r1))
        n0 = (d * over) * r0 - (b * over) * r1
        n1 = (a * over) * r1 - (c * over) * r0
        p = jnp.where((lane == k) | (lane == k + 1), 0.0, p) - c0 * n0 - c1 * n1
        p = jnp.where(row == k, n0, jnp.where(row == k + 1, n1, p))
    return p


def invert(e):
    order = e.shape[0]
    size = 32

    def step(s, carry):
        a = e[...]
        pivot = small_inverse(a[0:size, 0:size])
        right = dot(pivot, a[0:size, :])
        lane = iota((1, order), 1) < size
        corner = jnp.concatenate([pivot, jnp.zeros((size, order - size), F32)], 1)
        right = jnp.where(lane, corner, right)
        rest = jnp.where(lane, 0.0, a[size:, :]) - dot(a[size:, 0:size], right)
        e[0 : order - size, :] = pltpu.roll(rest, order - size, 1)
        e[order - size :, :] = pltpu.roll(right, order - size, 1)
        return carry

    lax.fori_loop(0, order // size, step, 0)


def column(g, num, order, offset, base):
    n = g.shape[0]
    pick = jnp.where(iota((order, n), 1) == lax.div(iota((order, n), 0), num) + offset, 1.0, 0.0)
    spread = dot(pick, g)
    lane, row = iota(spread.shape, 1), iota(spread.shape, 0)
    return jnp.sum(jnp.where(lane == base + lax.rem(row, num), spread, 0.0), axis=1, keepdims=True)


def matrix_from(got, num, across, e):
    order = e.shape[0]
    n = got.shape[0]
    square = num * num
    pick = jnp.where(iota((order, n), 1) == lax.div(iota((order, n), 0), num), 1.0, 0.0)
    lane, row = iota((order, 128), 1), iota((order, 128), 0)
    keep = lax.div(lax.rem(lane, square), num) == lax.rem(row, num)
    first = jnp.where(keep, dot(pick, got[:, 0, :]), 0.0)
    second = jnp.where(keep, dot(pick, got[:, 1, :]), 0.0)
    t, c = iota((128, order), 0), iota((128, order), 1)
    same = lax.rem(t, num) == lax.rem(c, num)
    low = jnp.where(same & (t < square), 1.0, 0.0)
    high = jnp.where(same & (t >= square), 1.0, 0.0)
    bi, bj = lax.div(iota((order, order), 0), num), lax.div(iota((order, order), 1), num)
    lower = jnp.where(bj == bi - across, dot(first, low), 0.0) + jnp.where(bj == bi - 1, dot(first, high), 0.0)
    e[...] = jnp.where(bi == bj, dot(second, low), 0.0) - lower - lower.T


def solve(e, col):
    return jnp.sum(e[...] * col, axis=0, keepdims=True)


def amounts(ids, solved, num, across):
    order = solved.shape[1]
    turned = pltpu.roll(jnp.broadcast_to(solved, (8, order)), ids[2], 1)
    take = lambda at: [turned[0:1, (at + k) % order : (at + k) % order + 1] for k in range(num)]
    return [take(at * num) for at in (0, -across, across, -1, 1)]


def combine(y, vectors):
    return functools.reduce(jnp.add, [c * v for c, v in zip(y, vectors)])


def spread_out(ys, z, zxl, zxh, zyl, zyh, gext, gy):
    num, nx, ny, nz = z.shape
    gext[0] = combine(ys[1], [zxl[k] for k in range(num)])
    gext[nx + 1] = combine(ys[2], [zxh[k] for k in range(num)])
    gy[0] = combine(ys[3], [zyl[k] for k in range(num)])
    gy[1] = combine(ys[4], [zyh[k] for k in range(num)])
    wide = [jnp.broadcast_to(c, (ny, nz)) for c in ys[0]]

    def plane(i, carry):
        gext[i + 1] = combine(wide, [z[k, i] for k in range(num)])
        return carry

    lax.fori_loop(0, nx, plane, 0)


def send_rows(i, p, evy, sy0, sy1):
    low, high = p[0:1, :], p[p.shape[0] - 1 :, :]
    sy0[pl.ds(i, 1), :] = jnp.where(evy, high, low)
    sy1[pl.ds(i, 1), :] = jnp.where(evy, low, high)


def send_planes(p, evx, sx0, sx1):
    low, high = p[0], p[p.shape[0] - 1]
    sx0[...] = jnp.where(evx, high, low)
    sx1[...] = jnp.where(evx, low, high)


def start_kernel(across, ids, got, x0, r0, z, zxl, zxh, zyl, zyh, fx, fyl, fyu, fzl, fzu, diag, dinv, e, x, r, p, sx0, sx1, sy0, sy1, gext, gy):
    num, nx, ny, nz = z.shape
    order = e.shape[0]
    matrix_from(got, num, across, e)
    invert(e)
    solved = solve(e, column(got[:, 1, :], num, order, 0, num * num))
    spread_out(amounts(ids, solved, num, across), z, zxl, zxh, zyl, zyh, gext, gy)
    faces = (fx, fyl, fyu, fzl, fzu, diag)
    evx, evy = ids[0] == 1, ids[1] == 1

    def plane(i, carry):
        g = gext[i + 1]
        image = act(i, g, gext[i], gext[i + 2], gy[0, pl.ds(i, 1), :], gy[1, pl.ds(i, 1), :], faces)
        x[i] = x0[i] + g
        rest = r0[i] - image
        r[i] = rest
        pre = rest * dinv[i]
        p[i] = pre
        send_rows(i, pre, evy, sy0, sy1)
        return carry

    lax.fori_loop(0, nx, plane, 0)
    send_planes(p, evx, sx0, sx1)


def product_kernel(first, *refs):
    ids, p, r, z, fx, fyl, fyu, fzl, fzu, diag, rx0, rx1, ry0, ry1 = refs[:14]
    applied = None if first else refs[14]
    ap, out, pext, py, acc = refs[-5:]
    num, nx, ny, nz = z.shape
    faces = (fx, fyl, fyu, fzl, fzu, diag)
    evx, evy = ids[0] == 1, ids[1] == 1
    pext[0] = jnp.where(evx, rx1[...], rx0[...])
    pext[nx + 1] = jnp.where(evx, rx0[...], rx1[...])
    py[0] = jnp.where(evy, ry1[...], ry0[...])
    py[1] = jnp.where(evy, ry0[...], ry1[...])
    acc[...] = jnp.zeros_like(acc)

    def fill(i, carry):
        pext[i + 1] = p[i]
        return carry

    lax.fori_loop(0, nx, fill, 0)

    def plane(i, carry):
        v = pext[i + 1]
        w = act(i, v, pext[i], pext[i + 2], py[0, pl.ds(i, 1), :], py[1, pl.ds(i, 1), :], faces)
        ap[i] = w
        add_to(acc, 0, v * r[i])
        add_to(acc, 1, v * w)
        if not first:
            add_to(acc, 2, v * applied[i])
        for k in range(num):
            add_to(acc, 3 + k, w * z[k, i])
        return carry

    lax.fori_loop(0, nx, plane, 0)
    out[:, 0, :] = jnp.broadcast_to(row_of(acc, acc.shape[0] // 8, 128), (out.shape[0], 128))


def update_kernel(first, last, across, *refs):
    ids, got, e, z, zxl, zxh, zyl, zyh, fx, fyl, fyu, fzl, fzu, diag, dinv, p, ap, x, r = refs[:19]
    at = 19
    if not first:
        d_old, ad_old, state_old = refs[at : at + 3]
        at += 3
    d, ad, x_new, r_new, p_new, state = refs[at : at + 6]
    at += 6
    if last:
        out, gext, gy, acc, py = refs[at:]
    else:
        sx0, sx1, sy0, sy1, gext, gy = refs[at:]
    num, nx, ny, nz = z.shape
    order = e.shape[0]
    faces = (fx, fyl, fyu, fzl, fzu, diag)
    g = got[:, 0, :]
    totals = jnp.sum(g, axis=0, keepdims=True)
    new, energy_p, cross = totals[:, 0:1], totals[:, 1:2], totals[:, 2:3]
    col = column(g, num, order, 0, 3)
    solved = solve(e, col)
    same = iota((order, order), 0) == iota((order, order), 1)
    line = jnp.sum(jnp.where(same, col, 0.0), axis=0, keepdims=True)
    energy = energy_p - jnp.sum(solved * line, axis=1, keepdims=True)
    if not first:
        beta = new / state_old[0:1, 0:1]
        energy = energy + 2.0 * beta * cross + beta * beta * state_old[1:2, 0:1]
        wide_beta = jnp.broadcast_to(beta, (ny, nz))
    step = jnp.broadcast_to(new / energy, (ny, nz))
    state[0:1, :] = jnp.broadcast_to(new, (1, 128))
    state[1:2, :] = jnp.broadcast_to(energy, (1, 128))
    state[2:8, :] = jnp.zeros((6, 128), F32)
    spread_out(amounts(ids, solved, num, across), z, zxl, zxh, zyl, zyh, gext, gy)
    evx, evy = ids[0] == 1, ids[1] == 1

    def plane(i, carry):
        c = gext[i + 1]
        image = act(i, c, gext[i], gext[i + 2], gy[0, pl.ds(i, 1), :], gy[1, pl.ds(i, 1), :], faces)
        way, acted = p[i] - c, ap[i] - image
        if not first:
            way, acted = way + wide_beta * d_old[i], acted + wide_beta * ad_old[i]
        d[i] = way
        ad[i] = acted
        x_new[i] = x[i] + step * way
        rest = r[i] - step * acted
        r_new[i] = rest
        pre = rest * dinv[i]
        p_new[i] = pre
        if last:
            add_to(acc, 0, rest * pre)
            py[0, pl.ds(i, 1), :] = pre[0:1, :] * fyl[i, 0:1, :]
            py[1, pl.ds(i, 1), :] = pre[ny - 1 : ny, :] * fyu[i, ny - 1 : ny, :]
        else:
            send_rows(i, pre, evy, sy0, sy1)
        return carry

    if last:
        acc[...] = jnp.zeros_like(acc)
    lax.fori_loop(0, nx, plane, 0)
    if not last:
        send_planes(p_new, evx, sx0, sx1)
        return
    row = iota((ny, nz), 0)

    def second(i, carry):
        v = p_new[i]
        left, right = beside_z(v)
        fa = jnp.where(i > 0, fx[i], 0.0)
        fb = jnp.where(i < nx - 1, fx[i + 1], 0.0)
        w = diag[i] * v - fa * p_new[jnp.maximum(i - 1, 0)] - fb * p_new[jnp.minimum(i + 1, nx - 1)]
        w = w - fzl[i] * left - fzu[i] * right - jnp.where(row == 0, 0.0, fyl[i]) * pltpu.roll(v, 1, 0)
        w = w - jnp.where(row == ny - 1, 0.0, fyu[i]) * pltpu.roll(v, ny - 1, 0)
        for k in range(num):
            add_to(acc, 8 + k, w * z[k, i])
        return carry

    lax.fori_loop(0, nx, second, 0)
    low, high = p_new[0] * fx[0], p_new[nx - 1] * fx[nx]
    for k in range(num):
        add_to(acc, 8 + num + k, -low * zxl[k])
        add_to(acc, 8 + 2 * num + k, -high * zxh[k])
        add_to(acc, 8 + 3 * num + k, -py[0] * zyl[k])
        add_to(acc, 8 + 4 * num + k, -py[1] * zyh[k])
    out[:, 0, :] = jnp.broadcast_to(row_of(acc, acc.shape[0] // 8, 128), (out.shape[0], 128))


def finish_kernel(across, ids, got, e, z, p, d_old, state_old, d):
    num, nx, ny, nz = z.shape
    order = e.shape[0]
    g = got[:, 0, :]
    beta = jnp.sum(g, axis=0, keepdims=True)[:, 0:1] / state_old[0:1, 0:1]
    col = column(g, num, order, 0, 8)
    for group, offset in ((1, across), (2, -across), (3, 1), (4, -1)):
        col = col + column(g, num, order, offset, 8 + group * num)
    ys = amounts(ids, solve(e, col), num, across)
    wide = [jnp.broadcast_to(c, (ny, nz)) for c in ys[0]]
    wide_beta = jnp.broadcast_to(beta, (ny, nz))

    def plane(i, carry):
        d[i] = p[i] + wide_beta * d_old[i] - combine(wide, [z[k, i] for k in range(num)])
        return carry

    lax.fori_loop(0, nx, plane, 0)


def call(kernel, name, args, outs, scratch):
    return pl.pallas_call(
        kernel,
        name=name,
        in_specs=[SMEM] + [VMEM] * (len(args) - 1),
        out_specs=[VMEM] * len(outs),
        out_shape=[jax.ShapeDtypeStruct(s, F32) for s in outs],
        scratch_shapes=[pltpu.VMEM(s, F32) for s in scratch],
        compiler_params=pltpu.CompilerParams(vmem_limit_bytes=48 * 1024 * 1024),
    )(*args)


def per_device(right_side, start_field, coef, deflation):
    num, nx, ny, nz = deflation.shape
    down, across = lax.axis_size("gx"), lax.axis_size("gy")
    n = down * across
    order = n * num
    ix, iy = lax.axis_index("gx"), lax.axis_index("gy")
    evx, evy = ix % 2 == 0, iy % 2 == 0
    ids = jnp.stack([evx.astype(jnp.int32), evy.astype(jnp.int32), (order - (ix * across + iy) * num) % order])

    def pack(at, index):
        return jnp.concatenate([at(coef, index)[None], at(start_field, index)[None], at(deflation, index)])

    at_x = lambda v, i: lax.dynamic_index_in_dim(v, i, v.ndim - 3, keepdims=False)
    at_y = lambda v, i: lax.dynamic_index_in_dim(v, i, v.ndim - 2, keepdims=False)
    xs = (jnp.where(evx, nx - 1, 0), jnp.where(evx, 0, nx - 1))
    ys = (jnp.where(evy, ny - 1, 0), jnp.where(evy, 0, ny - 1))
    raw = swaps([pack(at_x, xs[0]), pack(at_x, xs[1]), pack(at_y, ys[0]), pack(at_y, ys[1])])

    field, layer_x, layer_y = (nx, ny, nz), (ny, nz), (nx, nz)
    ext, two_y = (nx + 2, ny, nz), (2, nx, nz)
    layers = [layer_x, layer_x, layer_y, layer_y]
    wide = -(-(3 * num * num + num) // 128)
    *faces, dinv, r0, zxl, zxh, zyl, zyh, out = call(
        prepare_kernel,
        "prepare",
        [ids, right_side, start_field, coef, deflation, *raw],
        [(nx + 1, ny, nz)] + [field] * 7 + [(num,) + layer_x] * 2 + [(num,) + layer_y] * 2 + [(n, wide, 128)],
        [ext, ext, (4, nx, nz), (wide * 128 * 8, 128), (num, nx, nz)],
    )
    basis = [deflation, zxl, zxh, zyl, zyh]
    e, x, r, p, *sent = call(
        functools.partial(start_kernel, across),
        "start",
        [ids, everywhere(out), start_field, r0, *basis, *faces, dinv],
        [(order, order)] + [field] * 3 + layers,
        [ext, two_y],
    )
    old = []
    for iteration in range(ITERS):
        first, last = iteration == 0, iteration == ITERS - 1
        ap, out = call(
            functools.partial(product_kernel, first),
            "product",
            [ids, p, r, deflation, *faces, *swaps(sent)] + old[1:2],
            [field, (n, 1, 128)],
            [ext, two_y, (16 * 8, 128)],
        )
        d, ad, x, r, p, state, *sent = call(
            functools.partial(update_kernel, first, last, across),
            "update",
            [ids, everywhere(out), e, *basis, *faces, dinv, p, ap, x, r] + old,
            [field] * 5 + [(8, 128)] + ([(n, 1, 128)] if last else layers),
            [ext, two_y] + ([(48 * 8, 128), two_y] if last else []),
        )
        old = [d, ad, state]
    (direction,) = call(
        functools.partial(finish_kernel, across),
        "finish",
        [ids, everywhere(sent[0]), e, deflation, p, d, state],
        [field],
        [],
    )
    return x, r, direction


def solution(mesh):
    field = P("gx", "gy", None)
    return jax.shard_map(
        per_device,
        mesh=mesh,
        in_specs=(field, field, field, P(None, "gx", "gy", None)),
        out_specs=(field, field, field),
        check_vma=False,
    )
```

```python
import functools

import jax
import jax.numpy as jnp
from jax import lax
from jax.experimental import pallas as pl
from jax.experimental.pallas import tpu as pltpu
from jax.sharding import PartitionSpec as P

ITERS = 2
BOTH = ("gx", "gy")
HIGH = lax.Precision.HIGHEST
F32 = jnp.float32
VMEM = pl.BlockSpec(memory_space=pltpu.VMEM)
SMEM = pl.BlockSpec(memory_space=pltpu.SMEM)


def swap(value, axis, parity):
    count = lax.axis_size(axis)
    pairs = []
    for low in range(parity, count - 1, 2):
        pairs += [(low, low + 1), (low + 1, low)]
    return lax.ppermute(value, axis, pairs)


def swaps(layers):
    return [swap(v, axis, parity) for v, (axis, parity) in zip(layers, (("gx", 0), ("gx", 1), ("gy", 0), ("gy", 1)))]


def everywhere(payload):
    return lax.all_to_all(payload, BOTH, 0, 0)


def face(lower, upper):
    summed = lower + upper
    inside = (lower > 0.0) & (upper > 0.0)
    return jnp.where(inside, 2.0 * lower * upper / summed, summed)


def iota(shape, dim):
    return lax.broadcasted_iota(jnp.int32, shape, dim)


def dot(a, b):
    return lax.dot_general(a, b, (((1,), (0,)), ((), ())), precision=HIGH, preferred_element_type=F32)


def fold(x):
    pieces = [x[r : r + 8, c : c + 128] for r in range(0, x.shape[0], 8) for c in range(0, x.shape[1], 128)]
    return functools.reduce(jnp.add, pieces)


def row_of(acc, count, width):
    total = functools.reduce(jnp.add, [acc[pl.ds(s, count, stride=8), :] for s in range(8)])
    if width > count:
        total = jnp.concatenate([total, jnp.zeros((width - count, 128), F32)], 0)
    sums = lax.dot_general(jnp.ones((8, 128), F32), total, (((1,), (1,)), ((), ())), precision=HIGH, preferred_element_type=F32)
    return sums[0:1]


def add_to(acc, index, x):
    acc[pl.ds(index * 8, 8), :] += fold(x)


def beside_y(v, low, high):
    rows = v.shape[0]
    row = iota(v.shape, 0)
    below = jnp.where(row == 0, low, pltpu.roll(v, 1, 0))
    above = jnp.where(row == rows - 1, high, pltpu.roll(v, rows - 1, 0))
    return below, above


def beside_z(v):
    return pltpu.roll(v, 1, 1), pltpu.roll(v, v.shape[1] - 1, 1)


def act(i, v, before, after, low, high, faces):
    fx, fyl, fyu, fzl, fzu, diag = faces
    below, above = beside_y(v, low, high)
    left, right = beside_z(v)
    out = diag[i] * v - fx[i] * before - fx[i + 1] * after
    return out - fyl[i] * below - fyu[i] * above - fzl[i] * left - fzu[i] * right


def prepare_kernel(ids, b, x0, coef, z, rx0, rx1, ry0, ry1, fx, fyl, fyu, fzl, fzu, diag, dinv, r0, zxl, zxh, zyl, zyh, out, cext, xext, yrow, acc, zy0):
    num, nx, ny, nz = z.shape
    evx, evy = ids[0] == 1, ids[1] == 1
    cext[0] = jnp.where(evx, rx1[0], rx0[0])
    cext[nx + 1] = jnp.where(evx, rx0[0], rx1[0])
    xext[0] = jnp.where(evx, rx1[1], rx0[1])
    xext[nx + 1] = jnp.where(evx, rx0[1], rx1[1])
    for k in range(num):
        zxl[k] = jnp.where(evx, rx1[2 + k], rx0[2 + k])
        zxh[k] = jnp.where(evx, rx0[2 + k], rx1[2 + k])
        zyl[k] = jnp.where(evy, ry1[2 + k], ry0[2 + k])
        zyh[k] = jnp.where(evy, ry0[2 + k], ry1[2 + k])
    for f in range(2):
        yrow[2 * f] = jnp.where(evy, ry1[f], ry0[f])
        yrow[2 * f + 1] = jnp.where(evy, ry0[f], ry1[f])
    acc[...] = jnp.zeros_like(acc)

    def fill(i, carry):
        cext[i + 1] = coef[i]
        xext[i + 1] = x0[i]
        return carry

    lax.fori_loop(0, nx, fill, 0)

    def faces_x(i, carry):
        fx[i] = face(cext[i], cext[i + 1])
        return carry

    lax.fori_loop(0, nx + 1, faces_x, 0)
    lane, row = iota((ny, nz), 1), iota((ny, nz), 0)

    def faces_yz(i, carry):
        c = cext[i + 1]
        below, above = beside_y(c, yrow[0, pl.ds(i, 1), :], yrow[1, pl.ds(i, 1), :])
        left, right = beside_z(c)
        yl, yu = face(below, c), face(c, above)
        zl, zu = face(jnp.where(lane == 0, 0.0, left), c), face(c, jnp.where(lane == nz - 1, 0.0, right))
        d = fx[i + 1] + fx[i] + yu + yl + zu + zl
        fyl[i], fyu[i] = yl, yu
        fzl[i], fzu[i] = jnp.where(lane == 0, 0.0, zl), jnp.where(lane == nz - 1, 0.0, zu)
        diag[i] = d
        dinv[i] = 1.0 / d
        return carry

    lax.fori_loop(0, nx, faces_yz, 0)
    faces = (fx, fyl, fyu, fzl, fzu, diag)
    square = num * num

    def plane(i, carry):
        r = b[i] - act(i, xext[i + 1], xext[i], xext[i + 2], yrow[2, pl.ds(i, 1), :], yrow[3, pl.ds(i, 1), :], faces)
        r0[i] = r
        fa = jnp.where(i > 0, fx[i], 0.0)
        fb = jnp.where(i < nx - 1, fx[i + 1], 0.0)
        before, after = jnp.maximum(i - 1, 0), jnp.minimum(i + 1, nx - 1)
        yl, yu = jnp.where(row == 0, 0.0, fyl[i]), jnp.where(row == ny - 1, 0.0, fyu[i])
        for k in range(num):
            v = z[k, i]
            left, right = beside_z(v)
            w = diag[i] * v - fa * z[k, before] - fb * z[k, after] - fzl[i] * left - fzu[i] * right
            w = w - yl * pltpu.roll(v, 1, 0) - yu * pltpu.roll(v, ny - 1, 0)
            for m in range(k + 1):
                add_to(acc, 2 * square + m * num + k, w * z[m, i])
            add_to(acc, 3 * square + k, v * r)
            zy0[k, pl.ds(i, 1), :] = v[0:1, :] * fyl[i, 0:1, :]
        return carry

    lax.fori_loop(0, nx, plane, 0)
    for k in range(num):
        for m in range(k):
            acc[pl.ds((2 * square + k * num + m) * 8, 8), :] = acc[pl.ds((2 * square + m * num + k) * 8, 8), :]

    def below_blocks(k, carry):
        weighted = z[k, 0] * fx[0]
        for m in range(num):
            add_to(acc, k * num + m, weighted * zxl[m])
            add_to(acc, square + k * num + m, zy0[k] * zyl[m])
        return carry

    lax.fori_loop(0, num, below_blocks, 0)
    count = acc.shape[0] // 8
    line = row_of(acc, count, count)
    for part in range(count // 128):
        out[:, part, :] = jnp.broadcast_to(line[:, part * 128 : (part + 1) * 128], (out.shape[0], 128))


def levels(across):
    found, at, stride = [], 0, 1
    while stride < across:
        count = len(range(stride, across, 2 * stride))
        found.append((at, count, stride))
        at, stride = at + count, 2 * stride
    return found + [(at, 1, 0)]


def column_at(position, across):
    value = jnp.zeros_like(position)
    for at, count, stride in levels(across):
        value = jnp.where((position >= at) & (position < at + count), (position - at) * 2 * stride + stride, value)
    return value


def position_of(column_id, across):
    value = jnp.full_like(column_id, across - 1)
    for at, count, stride in levels(across)[:-1]:
        value = jnp.where(lax.rem(column_id, 2 * stride) == stride, at + lax.div(column_id, 2 * stride), value)
    return value


def device_of(index, num, down, across):
    across_id = column_at(lax.div(index, num * down), across)
    return lax.rem(lax.div(index, num), down) * across + across_id, across_id


def small_inverses(blocks, group=4):
    size = blocks[0].shape[0]
    lane, row, head = iota((size, size), 1), iota((size, size), 0), iota((1, size), 1)
    for start in range(0, size, group):
        wide = [[jnp.broadcast_to(p[:, k : k + 1], (size, size)) for k in range(start, start + group)] for p in blocks]
        for j in range(group):
            k = start + j
            for t, (p, cols) in enumerate(zip(blocks, wide)):
                over = 1.0 / cols[j][k : k + 1, :]
                line = jnp.where(head == k, 1.0, p[k : k + 1, :]) * over
                p = jnp.where(lane == k, 0.0, p) - cols[j] * line
                blocks[t] = jnp.where(row == k, line, p)
                for other in range(j + 1, group):
                    entry = cols[other][k : k + 1, :] * over
                    cols[other] = jnp.where(row == k, entry, cols[other] - cols[j] * entry)
    return blocks


def invert(e, size, across):
    order = e.shape[0]
    for at, count, _ in levels(across):
        low, width = at * size, count * size
        a = e[...]
        parts = small_inverses([a[low + t * size : low + (t + 1) * size, low + t * size : low + (t + 1) * size] for t in range(count)])
        zero = jnp.zeros((size, size), F32)
        pivot = jnp.concatenate([jnp.concatenate([parts[t] if t == u else zero for u in range(count)], 1) for t in range(count)], 0) if count > 1 else parts[0]
        lane = iota((width, order), 1)
        inside = (lane >= low) & (lane < low + width)
        unit = jnp.where(lane == iota((width, order), 0) + low, 1.0, 0.0)
        right = dot(pivot, jnp.where(inside, unit, a[low : low + width, :]))
        row, col = iota((order, order), 0), iota((order, order), 1)
        rest = jnp.where((col >= low) & (col < low + width), 0.0, a) - dot(a[:, low : low + width], right)
        e[...] = rest
        e[low : low + width, :] = right


def column(g, num, order, across, offset, base):
    n = g.shape[0]
    device, _ = device_of(iota((order, n), 0), num, n // across, across)
    pick = jnp.where(iota((order, n), 1) == device + offset, 1.0, 0.0)
    spread = dot(pick, g)
    lane, row = iota(spread.shape, 1), iota(spread.shape, 0)
    return jnp.sum(jnp.where(lane == base + lax.rem(row, num), spread, 0.0), axis=1, keepdims=True)


def matrix_from(got, num, across, e):
    order = e.shape[0]
    n = got.shape[0]
    square = num * num
    down = n // across
    device, _ = device_of(iota((order, n), 0), num, down, across)
    pick = jnp.where(iota((order, n), 1) == device, 1.0, 0.0)
    lane, row = iota((order, 128), 1), iota((order, 128), 0)
    keep = lax.div(lax.rem(lane, square), num) == lax.rem(row, num)
    first = jnp.where(keep, dot(pick, got[:, 0, :]), 0.0)
    second = jnp.where(keep, dot(pick, got[:, 1, :]), 0.0)
    t, c = iota((128, order), 0), iota((128, order), 1)
    same = lax.rem(t, num) == lax.rem(c, num)
    low = jnp.where(same & (t < square), 1.0, 0.0)
    high = jnp.where(same & (t >= square), 1.0, 0.0)
    bi, _ = device_of(iota((order, 1), 0), num, down, across)
    bj, _ = device_of(iota((1, order), 1), num, down, across)
    lower = jnp.where(bj == bi - across, dot(first, low), 0.0) + jnp.where(bj == bi - 1, dot(first, high), 0.0)
    e[...] = jnp.where(bi == bj, dot(second, low), 0.0) - lower - lower.T


def solve(e, col):
    return jnp.sum(e[...] * col, axis=0, keepdims=True)


def amounts(ids, solved, num):
    order = solved.shape[1]
    wide = jnp.broadcast_to(solved, (8, order))
    groups = [pltpu.roll(wide, ids[2 + group], 1) for group in range(5)]
    return [[turned[0:1, k : k + 1] for k in range(num)] for turned in groups]


def combine(y, vectors):
    return functools.reduce(jnp.add, [c * v for c, v in zip(y, vectors)])


def spread_out(ys, z, zxl, zxh, zyl, zyh, gext, gy):
    num, nx, ny, nz = z.shape
    gext[0] = combine(ys[1], [zxl[k] for k in range(num)])
    gext[nx + 1] = combine(ys[2], [zxh[k] for k in range(num)])
    gy[0] = combine(ys[3], [zyl[k] for k in range(num)])
    gy[1] = combine(ys[4], [zyh[k] for k in range(num)])
    wide = [jnp.broadcast_to(c, (ny, nz)) for c in ys[0]]

    def plane(i, carry):
        gext[i + 1] = combine(wide, [z[k, i] for k in range(num)])
        return carry

    lax.fori_loop(0, nx, plane, 0)


def send_rows(i, p, evy, sy0, sy1):
    low, high = p[0:1, :], p[p.shape[0] - 1 :, :]
    sy0[pl.ds(i, 1), :] = jnp.where(evy, high, low)
    sy1[pl.ds(i, 1), :] = jnp.where(evy, low, high)


def send_planes(p, evx, sx0, sx1):
    low, high = p[0], p[p.shape[0] - 1]
    sx0[...] = jnp.where(evx, high, low)
    sx1[...] = jnp.where(evx, low, high)


def start_kernel(across, ids, got, x0, r0, z, zxl, zxh, zyl, zyh, fx, fyl, fyu, fzl, fzu, diag, dinv, e, x, r, p, sx0, sx1, sy0, sy1, gext, gy):
    num, nx, ny, nz = z.shape
    order = e.shape[0]
    matrix_from(got, num, across, e)
    invert(e, got.shape[0] // across * num, across)
    solved = solve(e, column(got[:, 1, :], num, order, across, 0, num * num))
    spread_out(amounts(ids, solved, num), z, zxl, zxh, zyl, zyh, gext, gy)
    faces = (fx, fyl, fyu, fzl, fzu, diag)
    evx, evy = ids[0] == 1, ids[1] == 1

    def plane(i, carry):
        g = gext[i + 1]
        image = act(i, g, gext[i], gext[i + 2], gy[0, pl.ds(i, 1), :], gy[1, pl.ds(i, 1), :], faces)
        x[i] = x0[i] + g
        rest = r0[i] - image
        r[i] = rest
        pre = rest * dinv[i]
        p[i] = pre
        send_rows(i, pre, evy, sy0, sy1)
        return carry

    lax.fori_loop(0, nx, plane, 0)
    send_planes(p, evx, sx0, sx1)


def product_kernel(first, *refs):
    ids, p, r, z, fx, fyl, fyu, fzl, fzu, diag, rx0, rx1, ry0, ry1 = refs[:14]
    applied = None if first else refs[14]
    ap, out, pext, py, acc = refs[-5:]
    num, nx, ny, nz = z.shape
    faces = (fx, fyl, fyu, fzl, fzu, diag)
    evx, evy = ids[0] == 1, ids[1] == 1
    pext[0] = jnp.where(evx, rx1[...], rx0[...])
    pext[nx + 1] = jnp.where(evx, rx0[...], rx1[...])
    py[0] = jnp.where(evy, ry1[...], ry0[...])
    py[1] = jnp.where(evy, ry0[...], ry1[...])
    acc[...] = jnp.zeros_like(acc)

    def fill(i, carry):
        pext[i + 1] = p[i]
        return carry

    lax.fori_loop(0, nx, fill, 0)

    def plane(i, carry):
        v = pext[i + 1]
        w = act(i, v, pext[i], pext[i + 2], py[0, pl.ds(i, 1), :], py[1, pl.ds(i, 1), :], faces)
        ap[i] = w
        add_to(acc, 0, v * r[i])
        add_to(acc, 1, v * w)
        if not first:
            add_to(acc, 2, v * applied[i])
        for k in range(num):
            add_to(acc, 3 + k, w * z[k, i])
        return carry

    lax.fori_loop(0, nx, plane, 0)
    out[:, 0, :] = jnp.broadcast_to(row_of(acc, acc.shape[0] // 8, 128), (out.shape[0], 128))


def update_kernel(first, last, across, *refs):
    ids, got, e, z, zxl, zxh, zyl, zyh, fx, fyl, fyu, fzl, fzu, diag, dinv, p, ap, x, r = refs[:19]
    at = 19
    if not first:
        d_old, ad_old, state_old = refs[at : at + 3]
        at += 3
    d, ad, x_new, r_new, p_new, state = refs[at : at + 6]
    at += 6
    if last:
        out, gext, gy, acc, py = refs[at:]
    else:
        sx0, sx1, sy0, sy1, gext, gy = refs[at:]
    num, nx, ny, nz = z.shape
    order = e.shape[0]
    faces = (fx, fyl, fyu, fzl, fzu, diag)
    g = got[:, 0, :]
    totals = jnp.sum(g, axis=0, keepdims=True)
    new, energy_p, cross = totals[:, 0:1], totals[:, 1:2], totals[:, 2:3]
    col = column(g, num, order, across, 0, 3)
    solved = solve(e, col)
    same = iota((order, order), 0) == iota((order, order), 1)
    line = jnp.sum(jnp.where(same, col, 0.0), axis=0, keepdims=True)
    energy = energy_p - jnp.sum(solved * line, axis=1, keepdims=True)
    if not first:
        beta = new / state_old[0:1, 0:1]
        energy = energy + 2.0 * beta * cross + beta * beta * state_old[1:2, 0:1]
        wide_beta = jnp.broadcast_to(beta, (ny, nz))
    step = jnp.broadcast_to(new / energy, (ny, nz))
    state[0:1, :] = jnp.broadcast_to(new, (1, 128))
    state[1:2, :] = jnp.broadcast_to(energy, (1, 128))
    state[2:8, :] = jnp.zeros((6, 128), F32)
    spread_out(amounts(ids, solved, num), z, zxl, zxh, zyl, zyh, gext, gy)
    evx, evy = ids[0] == 1, ids[1] == 1

    def plane(i, carry):
        c = gext[i + 1]
        image = act(i, c, gext[i], gext[i + 2], gy[0, pl.ds(i, 1), :], gy[1, pl.ds(i, 1), :], faces)
        way, acted = p[i] - c, ap[i] - image
        if not first:
            way, acted = way + wide_beta * d_old[i], acted + wide_beta * ad_old[i]
        d[i] = way
        ad[i] = acted
        x_new[i] = x[i] + step * way
        rest = r[i] - step * acted
        r_new[i] = rest
        pre = rest * dinv[i]
        p_new[i] = pre
        if last:
            add_to(acc, 0, rest * pre)
            py[0, pl.ds(i, 1), :] = pre[0:1, :] * fyl[i, 0:1, :]
            py[1, pl.ds(i, 1), :] = pre[ny - 1 : ny, :] * fyu[i, ny - 1 : ny, :]
        else:
            send_rows(i, pre, evy, sy0, sy1)
        return carry

    if last:
        acc[...] = jnp.zeros_like(acc)
    lax.fori_loop(0, nx, plane, 0)
    if not last:
        send_planes(p_new, evx, sx0, sx1)
        return
    row = iota((ny, nz), 0)

    def second(i, carry):
        v = p_new[i]
        left, right = beside_z(v)
        fa = jnp.where(i > 0, fx[i], 0.0)
        fb = jnp.where(i < nx - 1, fx[i + 1], 0.0)
        w = diag[i] * v - fa * p_new[jnp.maximum(i - 1, 0)] - fb * p_new[jnp.minimum(i + 1, nx - 1)]
        w = w - fzl[i] * left - fzu[i] * right - jnp.where(row == 0, 0.0, fyl[i]) * pltpu.roll(v, 1, 0)
        w = w - jnp.where(row == ny - 1, 0.0, fyu[i]) * pltpu.roll(v, ny - 1, 0)
        for k in range(num):
            add_to(acc, 8 + k, w * z[k, i])
        return carry

    lax.fori_loop(0, nx, second, 0)
    low, high = p_new[0] * fx[0], p_new[nx - 1] * fx[nx]
    for k in range(num):
        add_to(acc, 8 + num + k, -low * zxl[k])
        add_to(acc, 8 + 2 * num + k, -high * zxh[k])
        add_to(acc, 8 + 3 * num + k, -py[0] * zyl[k])
        add_to(acc, 8 + 4 * num + k, -py[1] * zyh[k])
    out[:, 0, :] = jnp.broadcast_to(row_of(acc, acc.shape[0] // 8, 128), (out.shape[0], 128))


def finish_kernel(across, ids, got, e, z, p, d_old, state_old, d):
    num, nx, ny, nz = z.shape
    order = e.shape[0]
    g = got[:, 0, :]
    beta = jnp.sum(g, axis=0, keepdims=True)[:, 0:1] / state_old[0:1, 0:1]
    col = column(g, num, order, across, 0, 8)
    for group, offset in ((1, across), (2, -across), (3, 1), (4, -1)):
        col = col + column(g, num, order, across, offset, 8 + group * num)
    ys = amounts(ids, solve(e, col), num)
    wide = [jnp.broadcast_to(c, (ny, nz)) for c in ys[0]]
    wide_beta = jnp.broadcast_to(beta, (ny, nz))

    def plane(i, carry):
        d[i] = p[i] + wide_beta * d_old[i] - combine(wide, [z[k, i] for k in range(num)])
        return carry

    lax.fori_loop(0, nx, plane, 0)


def call(kernel, name, args, outs, scratch):
    return pl.pallas_call(
        kernel,
        name=name,
        in_specs=[SMEM] + [VMEM] * (len(args) - 1),
        out_specs=[VMEM] * len(outs),
        out_shape=[jax.ShapeDtypeStruct(s, F32) for s in outs],
        scratch_shapes=[pltpu.VMEM(s, F32) for s in scratch],
        compiler_params=pltpu.CompilerParams(vmem_limit_bytes=48 * 1024 * 1024),
    )(*args)


def per_device(right_side, start_field, coef, deflation):
    num, nx, ny, nz = deflation.shape
    down, across = lax.axis_size("gx"), lax.axis_size("gy")
    n = down * across
    order = n * num
    ix, iy = lax.axis_index("gx"), lax.axis_index("gy")
    evx, evy = ix % 2 == 0, iy % 2 == 0
    shifts = []
    for dx, dy in ((0, 0), (-1, 0), (1, 0), (0, -1), (0, 1)):
        place = position_of(jnp.clip(iy + dy, 0, across - 1), across) * down + jnp.clip(ix + dx, 0, down - 1)
        shifts.append((order - place * num) % order)
    ids = jnp.stack([evx.astype(jnp.int32), evy.astype(jnp.int32)] + shifts)

    def pack(at, index):
        return jnp.concatenate([at(coef, index)[None], at(start_field, index)[None], at(deflation, index)])

    at_x = lambda v, i: lax.dynamic_index_in_dim(v, i, v.ndim - 3, keepdims=False)
    at_y = lambda v, i: lax.dynamic_index_in_dim(v, i, v.ndim - 2, keepdims=False)
    xs = (jnp.where(evx, nx - 1, 0), jnp.where(evx, 0, nx - 1))
    ys = (jnp.where(evy, ny - 1, 0), jnp.where(evy, 0, ny - 1))
    raw = swaps([pack(at_x, xs[0]), pack(at_x, xs[1]), pack(at_y, ys[0]), pack(at_y, ys[1])])

    field, layer_x, layer_y = (nx, ny, nz), (ny, nz), (nx, nz)
    ext, two_y = (nx + 2, ny, nz), (2, nx, nz)
    layers = [layer_x, layer_x, layer_y, layer_y]
    wide = -(-(3 * num * num + num) // 128)
    *faces, dinv, r0, zxl, zxh, zyl, zyh, out = call(
        prepare_kernel,
        "prepare",
        [ids, right_side, start_field, coef, deflation, *raw],
        [(nx + 1, ny, nz)] + [field] * 7 + [(num,) + layer_x] * 2 + [(num,) + layer_y] * 2 + [(n, wide, 128)],
        [ext, ext, (4, nx, nz), (wide * 128 * 8, 128), (num, nx, nz)],
    )
    basis = [deflation, zxl, zxh, zyl, zyh]
    e, x, r, p, *sent = call(
        functools.partial(start_kernel, across),
        "start",
        [ids, everywhere(out), start_field, r0, *basis, *faces, dinv],
        [(order, order)] + [field] * 3 + layers,
        [ext, two_y],
    )
    old = []
    for iteration in range(ITERS):
        first, last = iteration == 0, iteration == ITERS - 1
        ap, out = call(
            functools.partial(product_kernel, first),
            "product",
            [ids, p, r, deflation, *faces, *swaps(sent)] + old[1:2],
            [field, (n, 1, 128)],
            [ext, two_y, (16 * 8, 128)],
        )
        d, ad, x, r, p, state, *sent = call(
            functools.partial(update_kernel, first, last, across),
            "update",
            [ids, everywhere(out), e, *basis, *faces, dinv, p, ap, x, r] + old,
            [field] * 5 + [(8, 128)] + ([(n, 1, 128)] if last else layers),
            [ext, two_y] + ([(48 * 8, 128), two_y] if last else []),
        )
        old = [d, ad, state]
    (direction,) = call(
        functools.partial(finish_kernel, across),
        "finish",
        [ids, everywhere(sent[0]), e, deflation, p, d, state],
        [field],
        [],
    )
    return x, r, direction


def solution(mesh):
    field = P("gx", "gy", None)
    return jax.shard_map(
        per_device,
        mesh=mesh,
        in_specs=(field, field, field, P(None, "gx", "gy", None)),
        out_specs=(field, field, field),
        check_vma=False,
    )
```

```python
import functools

import jax
import jax.numpy as jnp
from jax import lax
from jax.experimental import pallas as pl
from jax.experimental.pallas import tpu as pltpu
from jax.sharding import PartitionSpec as P

ITERS = 2
BOTH = ("gx", "gy")
HIGH = lax.Precision.HIGHEST
F32 = jnp.float32
VMEM = pl.BlockSpec(memory_space=pltpu.VMEM)
SMEM = pl.BlockSpec(memory_space=pltpu.SMEM)


def swap(value, axis, parity):
    count = lax.axis_size(axis)
    pairs = []
    for low in range(parity, count - 1, 2):
        pairs += [(low, low + 1), (low + 1, low)]
    return lax.ppermute(value, axis, pairs)


def swaps(layers):
    return [swap(v, axis, parity) for v, (axis, parity) in zip(layers, (("gx", 0), ("gx", 1), ("gy", 0), ("gy", 1)))]


def everywhere(payload):
    return lax.all_to_all(payload, BOTH, 0, 0)


def face(lower, upper):
    summed = lower + upper
    inside = (lower > 0.0) & (upper > 0.0)
    return jnp.where(inside, 2.0 * lower * upper / summed, summed)


def iota(shape, dim):
    return lax.broadcasted_iota(jnp.int32, shape, dim)


def dot(a, b):
    return lax.dot_general(a, b, (((1,), (0,)), ((), ())), precision=HIGH, preferred_element_type=F32)


def fold(x):
    pieces = [x[r : r + 8, c : c + 128] for r in range(0, x.shape[0], 8) for c in range(0, x.shape[1], 128)]
    return functools.reduce(jnp.add, pieces)


def row_of(acc, count, width):
    total = functools.reduce(jnp.add, [acc[pl.ds(s, count, stride=8), :] for s in range(8)])
    if width > count:
        total = jnp.concatenate([total, jnp.zeros((width - count, 128), F32)], 0)
    sums = lax.dot_general(jnp.ones((8, 128), F32), total, (((1,), (1,)), ((), ())), precision=HIGH, preferred_element_type=F32)
    return sums[0:1]


def add_to(acc, index, x):
    acc[pl.ds(index * 8, 8), :] += fold(x)


def beside_y(v, low, high):
    rows = v.shape[0]
    row = iota(v.shape, 0)
    below = jnp.where(row == 0, low, pltpu.roll(v, 1, 0))
    above = jnp.where(row == rows - 1, high, pltpu.roll(v, rows - 1, 0))
    return below, above


def beside_z(v):
    return pltpu.roll(v, 1, 1), pltpu.roll(v, v.shape[1] - 1, 1)


def act(i, v, before, after, low, high, faces):
    fx, fyl, fyu, fzl, fzu, diag = faces
    below, above = beside_y(v, low, high)
    left, right = beside_z(v)
    out = diag[i] * v - fx[i] * before - fx[i + 1] * after
    return out - fyl[i] * below - fyu[i] * above - fzl[i] * left - fzu[i] * right


def prepare_kernel(ids, b, x0, coef, z, rx0, rx1, ry0, ry1, fx, fyl, fyu, fzl, fzu, diag, dinv, r0, zxl, zxh, zyl, zyh, out, cext, xext, yrow, acc, zy0):
    num, nx, ny, nz = z.shape
    evx, evy = ids[0] == 1, ids[1] == 1
    cext[0] = jnp.where(evx, rx1[0], rx0[0])
    cext[nx + 1] = jnp.where(evx, rx0[0], rx1[0])
    xext[0] = jnp.where(evx, rx1[1], rx0[1])
    xext[nx + 1] = jnp.where(evx, rx0[1], rx1[1])
    for k in range(num):
        zxl[k] = jnp.where(evx, rx1[2 + k], rx0[2 + k])
        zxh[k] = jnp.where(evx, rx0[2 + k], rx1[2 + k])
        zyl[k] = jnp.where(evy, ry1[2 + k], ry0[2 + k])
        zyh[k] = jnp.where(evy, ry0[2 + k], ry1[2 + k])
    for f in range(2):
        yrow[2 * f] = jnp.where(evy, ry1[f], ry0[f])
        yrow[2 * f + 1] = jnp.where(evy, ry0[f], ry1[f])
    acc[...] = jnp.zeros_like(acc)

    def fill(i, carry):
        cext[i + 1] = coef[i]
        xext[i + 1] = x0[i]
        return carry

    lax.fori_loop(0, nx, fill, 0, unroll=4)

    def faces_x(i, carry):
        fx[i] = face(cext[i], cext[i + 1])
        return carry

    lax.fori_loop(0, nx + 1, faces_x, 0)
    lane, row = iota((ny, nz), 1), iota((ny, nz), 0)

    def faces_yz(i, carry):
        c = cext[i + 1]
        below, above = beside_y(c, yrow[0, pl.ds(i, 1), :], yrow[1, pl.ds(i, 1), :])
        left, right = beside_z(c)
        yl, yu = face(below, c), face(c, above)
        zl, zu = face(jnp.where(lane == 0, 0.0, left), c), face(c, jnp.where(lane == nz - 1, 0.0, right))
        d = fx[i + 1] + fx[i] + yu + yl + zu + zl
        fyl[i], fyu[i] = yl, yu
        fzl[i], fzu[i] = jnp.where(lane == 0, 0.0, zl), jnp.where(lane == nz - 1, 0.0, zu)
        diag[i] = d
        dinv[i] = 1.0 / d
        return carry

    lax.fori_loop(0, nx, faces_yz, 0, unroll=4)
    faces = (fx, fyl, fyu, fzl, fzu, diag)
    square = num * num

    def plane(i, carry):
        r = b[i] - act(i, xext[i + 1], xext[i], xext[i + 2], yrow[2, pl.ds(i, 1), :], yrow[3, pl.ds(i, 1), :], faces)
        r0[i] = r
        fa = jnp.where(i > 0, fx[i], 0.0)
        fb = jnp.where(i < nx - 1, fx[i + 1], 0.0)
        before, after = jnp.maximum(i - 1, 0), jnp.minimum(i + 1, nx - 1)
        yl, yu = jnp.where(row == 0, 0.0, fyl[i]), jnp.where(row == ny - 1, 0.0, fyu[i])
        for k in range(num):
            v = z[k, i]
            left, right = beside_z(v)
            w = diag[i] * v - fa * z[k, before] - fb * z[k, after] - fzl[i] * left - fzu[i] * right
            w = w - yl * pltpu.roll(v, 1, 0) - yu * pltpu.roll(v, ny - 1, 0)
            for m in range(k + 1):
                add_to(acc, 2 * square + m * num + k, w * z[m, i])
            add_to(acc, 3 * square + k, v * r)
            zy0[k, pl.ds(i, 1), :] = v[0:1, :] * fyl[i, 0:1, :]
        return carry

    lax.fori_loop(0, nx, plane, 0, unroll=4)
    for k in range(num):
        for m in range(k):
            acc[pl.ds((2 * square + k * num + m) * 8, 8), :] = acc[pl.ds((2 * square + m * num + k) * 8, 8), :]

    def below_blocks(k, carry):
        weighted = z[k, 0] * fx[0]
        for m in range(num):
            add_to(acc, k * num + m, weighted * zxl[m])
            add_to(acc, square + k * num + m, zy0[k] * zyl[m])
        return carry

    lax.fori_loop(0, num, below_blocks, 0)
    count = acc.shape[0] // 8
    line = row_of(acc, count, count)
    for part in range(count // 128):
        out[:, part, :] = jnp.broadcast_to(line[:, part * 128 : (part + 1) * 128], (out.shape[0], 128))


def levels(across):
    found, at, stride = [], 0, 1
    while stride < across:
        count = len(range(stride, across, 2 * stride))
        found.append((at, count, stride))
        at, stride = at + count, 2 * stride
    return found + [(at, 1, 0)]


def column_at(position, across):
    value = jnp.zeros_like(position)
    for at, count, stride in levels(across):
        value = jnp.where((position >= at) & (position < at + count), (position - at) * 2 * stride + stride, value)
    return value


def position_of(column_id, across):
    value = jnp.full_like(column_id, across - 1)
    for at, count, stride in levels(across)[:-1]:
        value = jnp.where(lax.rem(column_id, 2 * stride) == stride, at + lax.div(column_id, 2 * stride), value)
    return value


def device_of(index, num, down, across):
    across_id = column_at(lax.div(index, num * down), across)
    return lax.rem(lax.div(index, num), down) * across + across_id, across_id


def small_inverses(blocks, group=4):
    size = blocks[0].shape[0]
    lane, row, head = iota((size, size), 1), iota((size, size), 0), iota((1, size), 1)
    for start in range(0, size, group):
        wide = [[jnp.broadcast_to(p[:, k : k + 1], (size, size)) for k in range(start, start + group)] for p in blocks]
        for j in range(group):
            k = start + j
            for t, (p, cols) in enumerate(zip(blocks, wide)):
                over = 1.0 / cols[j][k : k + 1, :]
                line = jnp.where(head == k, 1.0, p[k : k + 1, :]) * over
                p = jnp.where(lane == k, 0.0, p) - cols[j] * line
                blocks[t] = jnp.where(row == k, line, p)
                for other in range(j + 1, group):
                    entry = cols[other][k : k + 1, :] * over
                    cols[other] = jnp.where(row == k, entry, cols[other] - cols[j] * entry)
    return blocks


def invert(e, size, across):
    order = e.shape[0]
    for at, count, _ in levels(across):
        low, width = at * size, count * size
        a = e[...]
        parts = small_inverses([a[low + t * size : low + (t + 1) * size, low + t * size : low + (t + 1) * size] for t in range(count)])
        zero = jnp.zeros((size, size), F32)
        pivot = jnp.concatenate([jnp.concatenate([parts[t] if t == u else zero for u in range(count)], 1) for t in range(count)], 0) if count > 1 else parts[0]
        lane = iota((width, order), 1)
        inside = (lane >= low) & (lane < low + width)
        unit = jnp.where(lane == iota((width, order), 0) + low, 1.0, 0.0)
        right = dot(pivot, jnp.where(inside, unit, a[low : low + width, :]))
        row, col = iota((order, order), 0), iota((order, order), 1)
        rest = jnp.where((col >= low) & (col < low + width), 0.0, a) - dot(a[:, low : low + width], right)
        e[...] = rest
        e[low : low + width, :] = right


def column(g, num, order, across, offset, base):
    n = g.shape[0]
    device, _ = device_of(iota((order, n), 0), num, n // across, across)
    pick = jnp.where(iota((order, n), 1) == device + offset, 1.0, 0.0)
    spread = dot(pick, g)
    lane, row = iota(spread.shape, 1), iota(spread.shape, 0)
    return jnp.sum(jnp.where(lane == base + lax.rem(row, num), spread, 0.0), axis=1, keepdims=True)


def matrix_from(got, num, across, e):
    order = e.shape[0]
    n = got.shape[0]
    square = num * num
    down = n // across
    device, _ = device_of(iota((order, n), 0), num, down, across)
    pick = jnp.where(iota((order, n), 1) == device, 1.0, 0.0)
    lane, row = iota((order, 128), 1), iota((order, 128), 0)
    keep = lax.div(lax.rem(lane, square), num) == lax.rem(row, num)
    first = jnp.where(keep, dot(pick, got[:, 0, :]), 0.0)
    second = jnp.where(keep, dot(pick, got[:, 1, :]), 0.0)
    t, c = iota((128, order), 0), iota((128, order), 1)
    same = lax.rem(t, num) == lax.rem(c, num)
    low = jnp.where(same & (t < square), 1.0, 0.0)
    high = jnp.where(same & (t >= square), 1.0, 0.0)
    bi, _ = device_of(iota((order, 1), 0), num, down, across)
    bj, _ = device_of(iota((1, order), 1), num, down, across)
    lower = jnp.where(bj == bi - across, dot(first, low), 0.0) + jnp.where(bj == bi - 1, dot(first, high), 0.0)
    e[...] = jnp.where(bi == bj, dot(second, low), 0.0) - lower - lower.T


def solve(e, col):
    return jnp.sum(e[...] * col, axis=0, keepdims=True)


def amounts(ids, solved, num):
    order = solved.shape[1]
    wide = jnp.broadcast_to(solved, (8, order))
    groups = [pltpu.roll(wide, ids[2 + group], 1) for group in range(5)]
    return [[turned[0:1, k : k + 1] for k in range(num)] for turned in groups]


def combine(y, vectors):
    return functools.reduce(jnp.add, [c * v for c, v in zip(y, vectors)])


def spread_out(ys, z, zxl, zxh, zyl, zyh, gext, gy):
    num, nx, ny, nz = z.shape
    gext[0] = combine(ys[1], [zxl[k] for k in range(num)])
    gext[nx + 1] = combine(ys[2], [zxh[k] for k in range(num)])
    gy[0] = combine(ys[3], [zyl[k] for k in range(num)])
    gy[1] = combine(ys[4], [zyh[k] for k in range(num)])
    wide = [jnp.broadcast_to(c, (ny, nz)) for c in ys[0]]

    def plane(i, carry):
        gext[i + 1] = combine(wide, [z[k, i] for k in range(num)])
        return carry

    lax.fori_loop(0, nx, plane, 0, unroll=4)


def send_rows(i, p, evy, sy0, sy1):
    low, high = p[0:1, :], p[p.shape[0] - 1 :, :]
    sy0[pl.ds(i, 1), :] = jnp.where(evy, high, low)
    sy1[pl.ds(i, 1), :] = jnp.where(evy, low, high)


def send_planes(p, evx, sx0, sx1):
    low, high = p[0], p[p.shape[0] - 1]
    sx0[...] = jnp.where(evx, high, low)
    sx1[...] = jnp.where(evx, low, high)


def start_kernel(across, ids, got, x0, r0, z, zxl, zxh, zyl, zyh, fx, fyl, fyu, fzl, fzu, diag, dinv, e, x, r, p, sx0, sx1, sy0, sy1, gext, gy):
    num, nx, ny, nz = z.shape
    order = e.shape[0]
    matrix_from(got, num, across, e)
    invert(e, got.shape[0] // across * num, across)
    solved = solve(e, column(got[:, 1, :], num, order, across, 0, num * num))
    spread_out(amounts(ids, solved, num), z, zxl, zxh, zyl, zyh, gext, gy)
    faces = (fx, fyl, fyu, fzl, fzu, diag)
    evx, evy = ids[0] == 1, ids[1] == 1

    def plane(i, carry):
        g = gext[i + 1]
        image = act(i, g, gext[i], gext[i + 2], gy[0, pl.ds(i, 1), :], gy[1, pl.ds(i, 1), :], faces)
        x[i] = x0[i] + g
        rest = r0[i] - image
        r[i] = rest
        pre = rest * dinv[i]
        p[i] = pre
        send_rows(i, pre, evy, sy0, sy1)
        return carry

    lax.fori_loop(0, nx, plane, 0, unroll=4)
    send_planes(p, evx, sx0, sx1)


def product_kernel(first, *refs):
    ids, p, r, z, fx, fyl, fyu, fzl, fzu, diag, rx0, rx1, ry0, ry1 = refs[:14]
    applied = None if first else refs[14]
    ap, out, pext, py, acc = refs[-5:]
    num, nx, ny, nz = z.shape
    faces = (fx, fyl, fyu, fzl, fzu, diag)
    evx, evy = ids[0] == 1, ids[1] == 1
    pext[0] = jnp.where(evx, rx1[...], rx0[...])
    pext[nx + 1] = jnp.where(evx, rx0[...], rx1[...])
    py[0] = jnp.where(evy, ry1[...], ry0[...])
    py[1] = jnp.where(evy, ry0[...], ry1[...])
    acc[...] = jnp.zeros_like(acc)

    def fill(i, carry):
        pext[i + 1] = p[i]
        return carry

    lax.fori_loop(0, nx, fill, 0, unroll=4)

    def plane(i, carry):
        v = pext[i + 1]
        w = act(i, v, pext[i], pext[i + 2], py[0, pl.ds(i, 1), :], py[1, pl.ds(i, 1), :], faces)
        ap[i] = w
        add_to(acc, 0, v * r[i])
        add_to(acc, 1, v * w)
        if not first:
            add_to(acc, 2, v * applied[i])
        for k in range(num):
            add_to(acc, 3 + k, w * z[k, i])
        return carry

    lax.fori_loop(0, nx, plane, 0, unroll=4)
    out[:, 0, :] = jnp.broadcast_to(row_of(acc, acc.shape[0] // 8, 128), (out.shape[0], 128))


def update_kernel(first, last, across, *refs):
    ids, got, e, z, zxl, zxh, zyl, zyh, fx, fyl, fyu, fzl, fzu, diag, dinv, p, ap, x, r = refs[:19]
    at = 19
    if not first:
        d_old, ad_old, state_old = refs[at : at + 3]
        at += 3
    d, ad, x_new, r_new, p_new, state = refs[at : at + 6]
    at += 6
    if last:
        out, gext, gy, acc, py = refs[at:]
    else:
        sx0, sx1, sy0, sy1, gext, gy = refs[at:]
    num, nx, ny, nz = z.shape
    order = e.shape[0]
    faces = (fx, fyl, fyu, fzl, fzu, diag)
    g = got[:, 0, :]
    totals = jnp.sum(g, axis=0, keepdims=True)
    new, energy_p, cross = totals[:, 0:1], totals[:, 1:2], totals[:, 2:3]
    col = column(g, num, order, across, 0, 3)
    solved = solve(e, col)
    same = iota((order, order), 0) == iota((order, order), 1)
    line = jnp.sum(jnp.where(same, col, 0.0), axis=0, keepdims=True)
    energy = energy_p - jnp.sum(solved * line, axis=1, keepdims=True)
    if not first:
        beta = new / state_old[0:1, 0:1]
        energy = energy + 2.0 * beta * cross + beta * beta * state_old[1:2, 0:1]
        wide_beta = jnp.broadcast_to(beta, (ny, nz))
    step = jnp.broadcast_to(new / energy, (ny, nz))
    state[0:1, :] = jnp.broadcast_to(new, (1, 128))
    state[1:2, :] = jnp.broadcast_to(energy, (1, 128))
    state[2:8, :] = jnp.zeros((6, 128), F32)
    spread_out(amounts(ids, solved, num), z, zxl, zxh, zyl, zyh, gext, gy)
    evx, evy = ids[0] == 1, ids[1] == 1

    def plane(i, carry):
        c = gext[i + 1]
        image = act(i, c, gext[i], gext[i + 2], gy[0, pl.ds(i, 1), :], gy[1, pl.ds(i, 1), :], faces)
        way, acted = p[i] - c, ap[i] - image
        if not first:
            way, acted = way + wide_beta * d_old[i], acted + wide_beta * ad_old[i]
        d[i] = way
        ad[i] = acted
        x_new[i] = x[i] + step * way
        rest = r[i] - step * acted
        r_new[i] = rest
        pre = rest * dinv[i]
        p_new[i] = pre
        if last:
            add_to(acc, 0, rest * pre)
            py[0, pl.ds(i, 1), :] = pre[0:1, :] * fyl[i, 0:1, :]
            py[1, pl.ds(i, 1), :] = pre[ny - 1 : ny, :] * fyu[i, ny - 1 : ny, :]
        else:
            send_rows(i, pre, evy, sy0, sy1)
        return carry

    if last:
        acc[...] = jnp.zeros_like(acc)
    lax.fori_loop(0, nx, plane, 0, unroll=4)
    if not last:
        send_planes(p_new, evx, sx0, sx1)
        return
    row = iota((ny, nz), 0)

    def second(i, carry):
        v = p_new[i]
        left, right = beside_z(v)
        fa = jnp.where(i > 0, fx[i], 0.0)
        fb = jnp.where(i < nx - 1, fx[i + 1], 0.0)
        w = diag[i] * v - fa * p_new[jnp.maximum(i - 1, 0)] - fb * p_new[jnp.minimum(i + 1, nx - 1)]
        w = w - fzl[i] * left - fzu[i] * right - jnp.where(row == 0, 0.0, fyl[i]) * pltpu.roll(v, 1, 0)
        w = w - jnp.where(row == ny - 1, 0.0, fyu[i]) * pltpu.roll(v, ny - 1, 0)
        for k in range(num):
            add_to(acc, 8 + k, w * z[k, i])
        return carry

    lax.fori_loop(0, nx, second, 0, unroll=4)
    low, high = p_new[0] * fx[0], p_new[nx - 1] * fx[nx]
    for k in range(num):
        add_to(acc, 8 + num + k, -low * zxl[k])
        add_to(acc, 8 + 2 * num + k, -high * zxh[k])
        add_to(acc, 8 + 3 * num + k, -py[0] * zyl[k])
        add_to(acc, 8 + 4 * num + k, -py[1] * zyh[k])
    out[:, 0, :] = jnp.broadcast_to(row_of(acc, acc.shape[0] // 8, 128), (out.shape[0], 128))


def finish_kernel(across, ids, got, e, z, p, d_old, state_old, d):
    num, nx, ny, nz = z.shape
    order = e.shape[0]
    g = got[:, 0, :]
    beta = jnp.sum(g, axis=0, keepdims=True)[:, 0:1] / state_old[0:1, 0:1]
    col = column(g, num, order, across, 0, 8)
    for group, offset in ((1, across), (2, -across), (3, 1), (4, -1)):
        col = col + column(g, num, order, across, offset, 8 + group * num)
    ys = amounts(ids, solve(e, col), num)
    wide = [jnp.broadcast_to(c, (ny, nz)) for c in ys[0]]
    wide_beta = jnp.broadcast_to(beta, (ny, nz))

    def plane(i, carry):
        d[i] = p[i] + wide_beta * d_old[i] - combine(wide, [z[k, i] for k in range(num)])
        return carry

    lax.fori_loop(0, nx, plane, 0, unroll=4)


def call(order, kernel, name, args, outs, scratch):
    return pl.pallas_call(
        kernel,
        name=name,
        in_specs=[SMEM] + [VMEM] * (len(args) - 1),
        out_specs=[VMEM] * len(outs),
        out_shape=[jax.ShapeDtypeStruct(s, F32) for s in outs],
        scratch_shapes=[pltpu.VMEM(s, F32) for s in scratch],
        compiler_params=pltpu.CompilerParams(vmem_limit_bytes=(16 << 20) + 32 * order * order),
    )(*args)


def per_device(right_side, start_field, coef, deflation):
    num, nx, ny, nz = deflation.shape
    down, across = lax.axis_size("gx"), lax.axis_size("gy")
    n = down * across
    order = n * num
    ix, iy = lax.axis_index("gx"), lax.axis_index("gy")
    evx, evy = ix % 2 == 0, iy % 2 == 0
    shifts = []
    for dx, dy in ((0, 0), (-1, 0), (1, 0), (0, -1), (0, 1)):
        place = position_of(jnp.clip(iy + dy, 0, across - 1), across) * down + jnp.clip(ix + dx, 0, down - 1)
        shifts.append((order - place * num) % order)
    ids = jnp.stack([evx.astype(jnp.int32), evy.astype(jnp.int32)] + shifts)

    def pack(at, index):
        return jnp.concatenate([at(coef, index)[None], at(start_field, index)[None], at(deflation, index)])

    at_x = lambda v, i: lax.dynamic_index_in_dim(v, i, v.ndim - 3, keepdims=False)
    at_y = lambda v, i: lax.dynamic_index_in_dim(v, i, v.ndim - 2, keepdims=False)
    xs = (jnp.where(evx, nx - 1, 0), jnp.where(evx, 0, nx - 1))
    ys = (jnp.where(evy, ny - 1, 0), jnp.where(evy, 0, ny - 1))
    raw = swaps([pack(at_x, xs[0]), pack(at_x, xs[1]), pack(at_y, ys[0]), pack(at_y, ys[1])])

    field, layer_x, layer_y = (nx, ny, nz), (ny, nz), (nx, nz)
    ext, two_y = (nx + 2, ny, nz), (2, nx, nz)
    layers = [layer_x, layer_x, layer_y, layer_y]
    wide = -(-(3 * num * num + num) // 128)
    *faces, dinv, r0, zxl, zxh, zyl, zyh, out = call(
        order,
        prepare_kernel,
        "prepare",
        [ids, right_side, start_field, coef, deflation, *raw],
        [(nx + 1, ny, nz)] + [field] * 7 + [(num,) + layer_x] * 2 + [(num,) + layer_y] * 2 + [(n, wide, 128)],
        [ext, ext, (4, nx, nz), (wide * 128 * 8, 128), (num, nx, nz)],
    )
    basis = [deflation, zxl, zxh, zyl, zyh]
    e, x, r, p, *sent = call(
        order,
        functools.partial(start_kernel, across),
        "start",
        [ids, everywhere(out), start_field, r0, *basis, *faces, dinv],
        [(order, order)] + [field] * 3 + layers,
        [ext, two_y],
    )
    old = []
    for iteration in range(ITERS):
        first, last = iteration == 0, iteration == ITERS - 1
        ap, out = call(
            order,
            functools.partial(product_kernel, first),
            "product",
            [ids, p, r, deflation, *faces, *swaps(sent)] + old[1:2],
            [field, (n, 1, 128)],
            [ext, two_y, (16 * 8, 128)],
        )
        d, ad, x, r, p, state, *sent = call(
            order,
            functools.partial(update_kernel, first, last, across),
            "update",
            [ids, everywhere(out), e, *basis, *faces, dinv, p, ap, x, r] + old,
            [field] * 5 + [(8, 128)] + ([(n, 1, 128)] if last else layers),
            [ext, two_y] + ([(48 * 8, 128), two_y] if last else []),
        )
        old = [d, ad, state]
    (direction,) = call(
        order,
        functools.partial(finish_kernel, across),
        "finish",
        [ids, everywhere(sent[0]), e, deflation, p, d, state],
        [field],
        [],
    )
    return x, r, direction


def solution(mesh):
    field = P("gx", "gy", None)
    return jax.shard_map(
        per_device,
        mesh=mesh,
        in_specs=(field, field, field, P(None, "gx", "gy", None)),
        out_specs=(field, field, field),
        check_vma=False,
    )
```

```python
import functools

import jax
import jax.numpy as jnp
from jax import lax
from jax.experimental import pallas as pl
from jax.experimental.pallas import tpu as pltpu
from jax.sharding import PartitionSpec as P

ITERS = 2
BOTH = ("gx", "gy")
HIGH = lax.Precision.HIGHEST
F32 = jnp.float32
VMEM = pl.BlockSpec(memory_space=pltpu.VMEM)
SMEM = pl.BlockSpec(memory_space=pltpu.SMEM)


def swap(value, axis, parity):
    count = lax.axis_size(axis)
    pairs = []
    for low in range(parity, count - 1, 2):
        pairs += [(low, low + 1), (low + 1, low)]
    return lax.ppermute(value, axis, pairs)


def swaps(layers):
    return [swap(v, axis, parity) for v, (axis, parity) in zip(layers, (("gx", 0), ("gx", 1), ("gy", 0), ("gy", 1)))]


def everywhere(payload):
    return lax.all_to_all(payload, BOTH, 0, 0)


def face(lower, upper):
    summed = lower + upper
    inside = (lower > 0.0) & (upper > 0.0)
    return jnp.where(inside, 2.0 * lower * upper / summed, summed)


def iota(shape, dim):
    return lax.broadcasted_iota(jnp.int32, shape, dim)


def dot(a, b):
    return lax.dot_general(a, b, (((1,), (0,)), ((), ())), precision=HIGH, preferred_element_type=F32)


def fold(x):
    pieces = [x[r : r + 8, c : c + 128] for r in range(0, x.shape[0], 8) for c in range(0, x.shape[1], 128)]
    return functools.reduce(jnp.add, pieces)


def row_of(acc, count, width):
    total = functools.reduce(jnp.add, [acc[pl.ds(s, count, stride=8), :] for s in range(8)])
    if width > count:
        total = jnp.concatenate([total, jnp.zeros((width - count, 128), F32)], 0)
    sums = lax.dot_general(jnp.ones((8, 128), F32), total, (((1,), (1,)), ((), ())), precision=HIGH, preferred_element_type=F32)
    return sums[0:1]


def add_to(acc, index, x):
    acc[pl.ds(index * 8, 8), :] += fold(x)


def beside_y(v, low, high):
    rows = v.shape[0]
    row = iota(v.shape, 0)
    below = jnp.where(row == 0, low, pltpu.roll(v, 1, 0))
    above = jnp.where(row == rows - 1, high, pltpu.roll(v, rows - 1, 0))
    return below, above


def beside_z(v):
    return pltpu.roll(v, 1, 1), pltpu.roll(v, v.shape[1] - 1, 1)


def act(i, v, before, after, low, high, faces):
    fx, fyl, fyu, fzl, fzu, diag = faces
    below, above = beside_y(v, low, high)
    left, right = beside_z(v)
    out = diag[i] * v - fx[i] * before - fx[i + 1] * after
    return out - fyl[i] * below - fyu[i] * above - fzl[i] * left - fzu[i] * right


def pack_kernel(ids, x0, coef, z, sx0, sx1, sy0, sy1):
    num, nx, ny, _ = z.shape
    evx, evy = ids[0] == 1, ids[1] == 1
    for f, ref in enumerate([coef, x0] + [z.at[k] for k in range(num)]):
        low, high = ref[0], ref[nx - 1]
        sx0[f], sx1[f] = jnp.where(evx, high, low), jnp.where(evx, low, high)
        low, high = ref[:, 0, :], ref[:, ny - 1, :]
        sy0[f], sy1[f] = jnp.where(evy, high, low), jnp.where(evy, low, high)


def prepare_kernel(ids, b, x0, coef, z, rx0, rx1, ry0, ry1, fx, fyl, fyu, fzl, fzu, diag, dinv, r0, zxl, zxh, zyl, zyh, out, cext, xext, yrow, acc, zy0):
    num, nx, ny, nz = z.shape
    evx, evy = ids[0] == 1, ids[1] == 1
    cext[0] = jnp.where(evx, rx1[0], rx0[0])
    cext[nx + 1] = jnp.where(evx, rx0[0], rx1[0])
    xext[0] = jnp.where(evx, rx1[1], rx0[1])
    xext[nx + 1] = jnp.where(evx, rx0[1], rx1[1])
    for k in range(num):
        zxl[k] = jnp.where(evx, rx1[2 + k], rx0[2 + k])
        zxh[k] = jnp.where(evx, rx0[2 + k], rx1[2 + k])
        zyl[k] = jnp.where(evy, ry1[2 + k], ry0[2 + k])
        zyh[k] = jnp.where(evy, ry0[2 + k], ry1[2 + k])
    for f in range(2):
        yrow[2 * f] = jnp.where(evy, ry1[f], ry0[f])
        yrow[2 * f + 1] = jnp.where(evy, ry0[f], ry1[f])
    acc[...] = jnp.zeros_like(acc)

    def fill(i, carry):
        cext[i + 1] = coef[i]
        xext[i + 1] = x0[i]
        return carry

    lax.fori_loop(0, nx, fill, 0, unroll=4)

    def faces_x(i, carry):
        fx[i] = face(cext[i], cext[i + 1])
        return carry

    lax.fori_loop(0, nx + 1, faces_x, 0)
    lane, deep, row = iota((ny, nz), 1), iota((ny, nz), 0), iota((8, nz), 0)

    def faces_yz(i, carry):
        c = cext[i + 1]
        below = jnp.where(deep == 0, yrow[0, pl.ds(i, 1), :], pltpu.roll(c, 1, 0))
        left, _ = beside_z(c)
        yl, zl = face(below, c), face(jnp.where(lane == 0, 0.0, left), c)
        edge = face(c[ny - 1 : ny, :], yrow[1, pl.ds(i, 1), :])
        yu = jnp.where(deep == ny - 1, edge, pltpu.roll(yl, ny - 1, 0))
        zu = jnp.where(lane == nz - 1, c, pltpu.roll(zl, nz - 1, 1))
        d = fx[i + 1] + fx[i] + yu + yl + zu + zl
        fyl[i], fyu[i] = yl, yu
        fzl[i], fzu[i] = jnp.where(lane == 0, 0.0, zl), jnp.where(lane == nz - 1, 0.0, zu)
        diag[i] = d
        dinv[i] = 1.0 / d
        return carry

    lax.fori_loop(0, nx, faces_yz, 0, unroll=4)
    faces = (fx, fyl, fyu, fzl, fzu, diag)
    square = num * num

    def plane(i, carry):
        r = b[i] - act(i, xext[i + 1], xext[i], xext[i + 2], yrow[2, pl.ds(i, 1), :], yrow[3, pl.ds(i, 1), :], faces)
        r0[i] = r
        before, after = jnp.maximum(i - 1, 0), jnp.minimum(i + 1, nx - 1)
        for s in range(0, ny, 8):
            rows = slice(s, s + 8)
            fa, fb = jnp.where(i > 0, fx[i, rows, :], 0.0), jnp.where(i < nx - 1, fx[i + 1, rows, :], 0.0)
            yl, yu, zl, zu, mid = fyl[i, rows, :], fyu[i, rows, :], fzl[i, rows, :], fzu[i, rows, :], diag[i, rows, :]
            yl = jnp.where(row == 0, 0.0, yl) if s == 0 else yl
            yu = jnp.where(row == 7, 0.0, yu) if s == ny - 8 else yu
            strips = [z[k, i, rows, :] for k in range(num)]
            for k, v in enumerate(strips):
                left, right = beside_z(v)
                below = z[k, i, s - 1 : s + 7, :] if s > 0 else pltpu.roll(v, 1, 0)
                above = z[k, i, s + 1 : s + 9, :] if s < ny - 8 else pltpu.roll(v, 7, 0)
                w = mid * v - fa * z[k, before, rows, :] - fb * z[k, after, rows, :]
                w = w - zl * left - zu * right - yl * below - yu * above
                for m in range(k + 1):
                    add_to(acc, 2 * square + m * num + k, w * strips[m])
                add_to(acc, 3 * square + k, v * r[rows, :])
        for k in range(num):
            zy0[k, pl.ds(i, 1), :] = z[k, i, 0:1, :] * fyl[i, 0:1, :]
        return carry

    lax.fori_loop(0, nx, plane, 0, unroll=4)
    for k in range(num):
        for m in range(k):
            acc[pl.ds((2 * square + k * num + m) * 8, 8), :] = acc[pl.ds((2 * square + m * num + k) * 8, 8), :]

    def below_blocks(k, carry):
        weighted = z[k, 0] * fx[0]
        for m in range(num):
            add_to(acc, k * num + m, weighted * zxl[m])
            add_to(acc, square + k * num + m, zy0[k] * zyl[m])
        return carry

    lax.fori_loop(0, num, below_blocks, 0)
    count = acc.shape[0] // 8
    line = row_of(acc, count, count)
    for part in range(count // 128):
        out[:, part, :] = jnp.broadcast_to(line[:, part * 128 : (part + 1) * 128], (out.shape[0], 128))


def levels(across):
    found, at, stride = [], 0, 1
    while stride < across:
        count = len(range(stride, across, 2 * stride))
        found.append((at, count, stride))
        at, stride = at + count, 2 * stride
    return found + [(at, 1, 0)]


def column_at(position, across):
    value = jnp.zeros_like(position)
    for at, count, stride in levels(across):
        value = jnp.where((position >= at) & (position < at + count), (position - at) * 2 * stride + stride, value)
    return value


def position_of(column_id, across):
    value = jnp.full_like(column_id, across - 1)
    for at, count, stride in levels(across)[:-1]:
        value = jnp.where(lax.rem(column_id, 2 * stride) == stride, at + lax.div(column_id, 2 * stride), value)
    return value


def device_of(index, num, down, across):
    across_id = column_at(lax.div(index, num * down), across)
    return lax.rem(lax.div(index, num), down) * across + across_id, across_id


def small_inverses(blocks, group=8):
    size = blocks[0].shape[0]
    lane, row, head = iota((size, size), 1), iota((size, size), 0), iota((1, size), 1)
    for start in range(0, size, group):
        wide = [[jnp.broadcast_to(p[:, k : k + 1], (size, size)) for k in range(start, start + group)] for p in blocks]
        for j in range(group):
            k = start + j
            for t, (p, cols) in enumerate(zip(blocks, wide)):
                over = 1.0 / cols[j][k : k + 1, :]
                line = jnp.where(head == k, 1.0, p[k : k + 1, :]) * over
                p = jnp.where(lane == k, 0.0, p) - cols[j] * line
                blocks[t] = jnp.where(row == k, line, p)
                for other in range(j + 1, group):
                    entry = cols[other][k : k + 1, :] * over
                    cols[other] = jnp.where(row == k, entry, cols[other] - cols[j] * entry)
    return blocks


def invert(e, size, across):
    order = e.shape[0]
    for at, count, _ in levels(across):
        low, width = at * size, count * size
        a = e[...]
        parts = small_inverses([a[low + t * size : low + (t + 1) * size, low + t * size : low + (t + 1) * size] for t in range(count)])
        zero = jnp.zeros((size, size), F32)
        pivot = jnp.concatenate([jnp.concatenate([parts[t] if t == u else zero for u in range(count)], 1) for t in range(count)], 0) if count > 1 else parts[0]
        lane = iota((width, order), 1)
        inside = (lane >= low) & (lane < low + width)
        unit = jnp.where(lane == iota((width, order), 0) + low, 1.0, 0.0)
        right = dot(pivot, jnp.where(inside, unit, a[low : low + width, :]))
        row, col = iota((order, order), 0), iota((order, order), 1)
        rest = jnp.where((col >= low) & (col < low + width), 0.0, a) - dot(a[:, low : low + width], right)
        e[...] = rest
        e[low : low + width, :] = right


def column(g, num, order, across, offset, base):
    n = g.shape[0]
    device, _ = device_of(iota((order, n), 0), num, n // across, across)
    pick = jnp.where(iota((order, n), 1) == device + offset, 1.0, 0.0)
    spread = dot(pick, g)
    lane, row = iota(spread.shape, 1), iota(spread.shape, 0)
    return jnp.sum(jnp.where(lane == base + lax.rem(row, num), spread, 0.0), axis=1, keepdims=True)


def matrix_from(got, num, across, e):
    order = e.shape[0]
    n = got.shape[0]
    square = num * num
    down = n // across
    device, _ = device_of(iota((order, n), 0), num, down, across)
    pick = jnp.where(iota((order, n), 1) == device, 1.0, 0.0)
    lane, row = iota((order, 128), 1), iota((order, 128), 0)
    keep = lax.div(lax.rem(lane, square), num) == lax.rem(row, num)
    first = jnp.where(keep, dot(pick, got[:, 0, :]), 0.0)
    second = jnp.where(keep, dot(pick, got[:, 1, :]), 0.0)
    t, c = iota((128, order), 0), iota((128, order), 1)
    same = lax.rem(t, num) == lax.rem(c, num)
    low = jnp.where(same & (t < square), 1.0, 0.0)
    high = jnp.where(same & (t >= square), 1.0, 0.0)
    bi, _ = device_of(iota((order, 1), 0), num, down, across)
    bj, _ = device_of(iota((1, order), 1), num, down, across)
    lower = jnp.where(bj == bi - across, dot(first, low), 0.0) + jnp.where(bj == bi - 1, dot(first, high), 0.0)
    e[...] = jnp.where(bi == bj, dot(second, low), 0.0) - lower - lower.T


def solve(e, col):
    return jnp.sum(e[...] * col, axis=0, keepdims=True)


def amounts(ids, solved, num):
    order = solved.shape[1]
    wide = jnp.broadcast_to(solved, (8, order))
    groups = [pltpu.roll(wide, ids[2 + group], 1) for group in range(5)]
    return [[turned[0:1, k : k + 1] for k in range(num)] for turned in groups]


def combine(y, vectors):
    return functools.reduce(jnp.add, [c * v for c, v in zip(y, vectors)])


def spread_out(ys, z, zxl, zxh, zyl, zyh, gext, gy):
    num, nx, ny, nz = z.shape
    gext[0] = combine(ys[1], [zxl[k] for k in range(num)])
    gext[nx + 1] = combine(ys[2], [zxh[k] for k in range(num)])
    gy[0] = combine(ys[3], [zyl[k] for k in range(num)])
    gy[1] = combine(ys[4], [zyh[k] for k in range(num)])
    wide = [jnp.broadcast_to(c, (ny, nz)) for c in ys[0]]

    def plane(i, carry):
        gext[i + 1] = combine(wide, [z[k, i] for k in range(num)])
        return carry

    lax.fori_loop(0, nx, plane, 0, unroll=4)


def send_rows(i, p, evy, sy0, sy1):
    low, high = p[0:1, :], p[p.shape[0] - 1 :, :]
    sy0[pl.ds(i, 1), :] = jnp.where(evy, high, low)
    sy1[pl.ds(i, 1), :] = jnp.where(evy, low, high)


def send_planes(p, evx, sx0, sx1):
    low, high = p[0], p[p.shape[0] - 1]
    sx0[...] = jnp.where(evx, high, low)
    sx1[...] = jnp.where(evx, low, high)


def start_kernel(across, ids, got, x0, r0, z, zxl, zxh, zyl, zyh, fx, fyl, fyu, fzl, fzu, diag, dinv, e, x, r, p, sx0, sx1, sy0, sy1, gext, gy):
    num, nx, ny, nz = z.shape
    order = e.shape[0]
    matrix_from(got, num, across, e)
    invert(e, got.shape[0] // across * num, across)
    solved = solve(e, column(got[:, 1, :], num, order, across, 0, num * num))
    spread_out(amounts(ids, solved, num), z, zxl, zxh, zyl, zyh, gext, gy)
    faces = (fx, fyl, fyu, fzl, fzu, diag)
    evx, evy = ids[0] == 1, ids[1] == 1

    def plane(i, carry):
        g = gext[i + 1]
        image = act(i, g, gext[i], gext[i + 2], gy[0, pl.ds(i, 1), :], gy[1, pl.ds(i, 1), :], faces)
        x[i] = x0[i] + g
        rest = r0[i] - image
        r[i] = rest
        pre = rest * dinv[i]
        p[i] = pre
        send_rows(i, pre, evy, sy0, sy1)
        return carry

    lax.fori_loop(0, nx, plane, 0, unroll=4)
    send_planes(p, evx, sx0, sx1)


def product_kernel(first, *refs):
    ids, p, r, z, fx, fyl, fyu, fzl, fzu, diag, rx0, rx1, ry0, ry1 = refs[:14]
    applied = None if first else refs[14]
    ap, out, pext, py, acc = refs[-5:]
    num, nx, ny, nz = z.shape
    faces = (fx, fyl, fyu, fzl, fzu, diag)
    evx, evy = ids[0] == 1, ids[1] == 1
    pext[0] = jnp.where(evx, rx1[...], rx0[...])
    pext[nx + 1] = jnp.where(evx, rx0[...], rx1[...])
    py[0] = jnp.where(evy, ry1[...], ry0[...])
    py[1] = jnp.where(evy, ry0[...], ry1[...])
    acc[...] = jnp.zeros_like(acc)

    def fill(i, carry):
        pext[i + 1] = p[i]
        return carry

    lax.fori_loop(0, nx, fill, 0, unroll=4)

    def plane(i, carry):
        v = pext[i + 1]
        w = act(i, v, pext[i], pext[i + 2], py[0, pl.ds(i, 1), :], py[1, pl.ds(i, 1), :], faces)
        ap[i] = w
        add_to(acc, 0, v * r[i])
        add_to(acc, 1, v * w)
        if not first:
            add_to(acc, 2, v * applied[i])
        for k in range(num):
            add_to(acc, 3 + k, w * z[k, i])
        return carry

    lax.fori_loop(0, nx, plane, 0, unroll=4)
    out[:, 0, :] = jnp.broadcast_to(row_of(acc, acc.shape[0] // 8, 128), (out.shape[0], 128))


def update_kernel(first, last, across, *refs):
    ids, got, e, z, zxl, zxh, zyl, zyh, fx, fyl, fyu, fzl, fzu, diag, dinv, p, ap, x, r = refs[:19]
    at = 19
    if not first:
        d_old, ad_old, state_old = refs[at : at + 3]
        at += 3
    d, ad, x_new, r_new, p_new, state = refs[at : at + 6]
    at += 6
    if last:
        out, gext, gy, acc, py = refs[at:]
    else:
        sx0, sx1, sy0, sy1, gext, gy = refs[at:]
    num, nx, ny, nz = z.shape
    order = e.shape[0]
    faces = (fx, fyl, fyu, fzl, fzu, diag)
    g = got[:, 0, :]
    totals = jnp.sum(g, axis=0, keepdims=True)
    new, energy_p, cross = totals[:, 0:1], totals[:, 1:2], totals[:, 2:3]
    col = column(g, num, order, across, 0, 3)
    solved = solve(e, col)
    same = iota((order, order), 0) == iota((order, order), 1)
    line = jnp.sum(jnp.where(same, col, 0.0), axis=0, keepdims=True)
    energy = energy_p - jnp.sum(solved * line, axis=1, keepdims=True)
    if not first:
        beta = new / state_old[0:1, 0:1]
        energy = energy + 2.0 * beta * cross + beta * beta * state_old[1:2, 0:1]
        wide_beta = jnp.broadcast_to(beta, (ny, nz))
    step = jnp.broadcast_to(new / energy, (ny, nz))
    state[0:1, :] = jnp.broadcast_to(new, (1, 128))
    state[1:2, :] = jnp.broadcast_to(energy, (1, 128))
    state[2:8, :] = jnp.zeros((6, 128), F32)
    spread_out(amounts(ids, solved, num), z, zxl, zxh, zyl, zyh, gext, gy)
    evx, evy = ids[0] == 1, ids[1] == 1

    def plane(i, carry):
        c = gext[i + 1]
        image = act(i, c, gext[i], gext[i + 2], gy[0, pl.ds(i, 1), :], gy[1, pl.ds(i, 1), :], faces)
        way, acted = p[i] - c, ap[i] - image
        if not first:
            way, acted = way + wide_beta * d_old[i], acted + wide_beta * ad_old[i]
        d[i] = way
        ad[i] = acted
        x_new[i] = x[i] + step * way
        rest = r[i] - step * acted
        r_new[i] = rest
        pre = rest * dinv[i]
        p_new[i] = pre
        if last:
            add_to(acc, 0, rest * pre)
            py[0, pl.ds(i, 1), :] = pre[0:1, :] * fyl[i, 0:1, :]
            py[1, pl.ds(i, 1), :] = pre[ny - 1 : ny, :] * fyu[i, ny - 1 : ny, :]
        else:
            send_rows(i, pre, evy, sy0, sy1)
        return carry

    if last:
        acc[...] = jnp.zeros_like(acc)
    lax.fori_loop(0, nx, plane, 0, unroll=4)
    if not last:
        send_planes(p_new, evx, sx0, sx1)
        return
    row = iota((ny, nz), 0)

    def second(i, carry):
        v = p_new[i]
        left, right = beside_z(v)
        fa = jnp.where(i > 0, fx[i], 0.0)
        fb = jnp.where(i < nx - 1, fx[i + 1], 0.0)
        w = diag[i] * v - fa * p_new[jnp.maximum(i - 1, 0)] - fb * p_new[jnp.minimum(i + 1, nx - 1)]
        w = w - fzl[i] * left - fzu[i] * right - jnp.where(row == 0, 0.0, fyl[i]) * pltpu.roll(v, 1, 0)
        w = w - jnp.where(row == ny - 1, 0.0, fyu[i]) * pltpu.roll(v, ny - 1, 0)
        for k in range(num):
            add_to(acc, 8 + k, w * z[k, i])
        return carry

    lax.fori_loop(0, nx, second, 0, unroll=4)
    low, high = p_new[0] * fx[0], p_new[nx - 1] * fx[nx]
    for k in range(num):
        add_to(acc, 8 + num + k, -low * zxl[k])
        add_to(acc, 8 + 2 * num + k, -high * zxh[k])
        add_to(acc, 8 + 3 * num + k, -py[0] * zyl[k])
        add_to(acc, 8 + 4 * num + k, -py[1] * zyh[k])
    out[:, 0, :] = jnp.broadcast_to(row_of(acc, acc.shape[0] // 8, 128), (out.shape[0], 128))


def finish_kernel(across, ids, got, e, z, p, d_old, state_old, d):
    num, nx, ny, nz = z.shape
    order = e.shape[0]
    g = got[:, 0, :]
    beta = jnp.sum(g, axis=0, keepdims=True)[:, 0:1] / state_old[0:1, 0:1]
    parts, n = g, g.shape[0]
    for group, offset in ((1, across), (2, -across), (3, 1), (4, -1)):
        moved = pltpu.roll(pltpu.roll(g, (n - offset) % n, 0), 128 - group * num, 1)
        parts = parts + moved
    ys = amounts(ids, solve(e, column(parts, num, order, across, 0, 8)), num)
    wide = [jnp.broadcast_to(c, (ny, nz)) for c in ys[0]]
    wide_beta = jnp.broadcast_to(beta, (ny, nz))

    def plane(i, carry):
        d[i] = p[i] + wide_beta * d_old[i] - combine(wide, [z[k, i] for k in range(num)])
        return carry

    lax.fori_loop(0, nx, plane, 0, unroll=4)


def call(order, kernel, name, args, outs, scratch):
    return pl.pallas_call(
        kernel,
        name=name,
        in_specs=[SMEM] + [VMEM] * (len(args) - 1),
        out_specs=[VMEM] * len(outs),
        out_shape=[jax.ShapeDtypeStruct(s, F32) for s in outs],
        scratch_shapes=[pltpu.VMEM(s, F32) for s in scratch],
        compiler_params=pltpu.CompilerParams(vmem_limit_bytes=(16 << 20) + 32 * order * order),
    )(*args)


def per_device(right_side, start_field, coef, deflation):
    num, nx, ny, nz = deflation.shape
    down, across = lax.axis_size("gx"), lax.axis_size("gy")
    n = down * across
    order = n * num
    ix, iy = lax.axis_index("gx"), lax.axis_index("gy")
    evx, evy = ix % 2 == 0, iy % 2 == 0
    shifts = []
    for dx, dy in ((0, 0), (-1, 0), (1, 0), (0, -1), (0, 1)):
        place = position_of(jnp.clip(iy + dy, 0, across - 1), across) * down + jnp.clip(ix + dx, 0, down - 1)
        shifts.append((order - place * num) % order)
    ids = jnp.stack([evx.astype(jnp.int32), evy.astype(jnp.int32)] + shifts)

    field, layer_x, layer_y = (nx, ny, nz), (ny, nz), (nx, nz)
    ext, two_y = (nx + 2, ny, nz), (2, nx, nz)
    layers = [layer_x, layer_x, layer_y, layer_y]
    raw = swaps(
        call(
            order,
            pack_kernel,
            "pack",
            [ids, start_field, coef, deflation],
            [(2 + num,) + layer_x] * 2 + [(2 + num,) + layer_y] * 2,
            [],
        )
    )
    wide = -(-(3 * num * num + num) // 128)
    *faces, dinv, r0, zxl, zxh, zyl, zyh, out = call(
        order,
        prepare_kernel,
        "prepare",
        [ids, right_side, start_field, coef, deflation, *raw],
        [(nx + 1, ny, nz)] + [field] * 7 + [(num,) + layer_x] * 2 + [(num,) + layer_y] * 2 + [(n, wide, 128)],
        [ext, ext, (4, nx, nz), (wide * 128 * 8, 128), (num, nx, nz)],
    )
    basis = [deflation, zxl, zxh, zyl, zyh]
    e, x, r, p, *sent = call(
        order,
        functools.partial(start_kernel, across),
        "start",
        [ids, everywhere(out), start_field, r0, *basis, *faces, dinv],
        [(order, order)] + [field] * 3 + layers,
        [ext, two_y],
    )
    old = []
    for iteration in range(ITERS):
        first, last = iteration == 0, iteration == ITERS - 1
        ap, out = call(
            order,
            functools.partial(product_kernel, first),
            "product",
            [ids, p, r, deflation, *faces, *swaps(sent)] + old[1:2],
            [field, (n, 1, 128)],
            [ext, two_y, (16 * 8, 128)],
        )
        d, ad, x, r, p, state, *sent = call(
            order,
            functools.partial(update_kernel, first, last, across),
            "update",
            [ids, everywhere(out), e, *basis, *faces, dinv, p, ap, x, r] + old,
            [field] * 5 + [(8, 128)] + ([(n, 1, 128)] if last else layers),
            [ext, two_y] + ([(48 * 8, 128), two_y] if last else []),
        )
        old = [d, ad, state]
    (direction,) = call(
        order,
        functools.partial(finish_kernel, across),
        "finish",
        [ids, everywhere(sent[0]), e, deflation, p, d, state],
        [field],
        [],
    )
    return x, r, direction


def solution(mesh):
    field = P("gx", "gy", None)
    return jax.shard_map(
        per_device,
        mesh=mesh,
        in_specs=(field, field, field, P(None, "gx", "gy", None)),
        out_specs=(field, field, field),
        check_vma=False,
    )
```

```python
import functools

import jax
import jax.numpy as jnp
from jax import lax
from jax.experimental import pallas as pl
from jax.experimental.pallas import tpu as pltpu
from jax.sharding import PartitionSpec as P

ITERS = 2
BOTH = ("gx", "gy")
HIGH = lax.Precision.HIGHEST
F32 = jnp.float32
VMEM = pl.BlockSpec(memory_space=pltpu.VMEM)
SMEM = pl.BlockSpec(memory_space=pltpu.SMEM)


def swap(value, axis, parity):
    count = lax.axis_size(axis)
    pairs = []
    for low in range(parity, count - 1, 2):
        pairs += [(low, low + 1), (low + 1, low)]
    return lax.ppermute(value, axis, pairs)


def swaps(layers):
    return [swap(v, axis, parity) for v, (axis, parity) in zip(layers, (("gx", 0), ("gx", 1), ("gy", 0), ("gy", 1)))]


def everywhere(payload):
    return lax.all_to_all(payload, BOTH, 0, 0)


def face(lower, upper):
    summed = lower + upper
    inside = (lower > 0.0) & (upper > 0.0)
    return jnp.where(inside, 2.0 * lower * upper / summed, summed)


def iota(shape, dim):
    return lax.broadcasted_iota(jnp.int32, shape, dim)


def dot(a, b):
    return lax.dot_general(a, b, (((1,), (0,)), ((), ())), precision=HIGH, preferred_element_type=F32)


def fold(x):
    pieces = [x[r : r + 8, c : c + 128] for r in range(0, x.shape[0], 8) for c in range(0, x.shape[1], 128)]
    return functools.reduce(jnp.add, pieces)


def row_of(acc, count, width):
    total = functools.reduce(jnp.add, [acc[pl.ds(s, count, stride=8), :] for s in range(8)])
    if width > count:
        total = jnp.concatenate([total, jnp.zeros((width - count, 128), F32)], 0)
    sums = lax.dot_general(jnp.ones((8, 128), F32), total, (((1,), (1,)), ((), ())), precision=HIGH, preferred_element_type=F32)
    return sums[0:1]


def add_to(acc, index, x):
    acc[pl.ds(index * 8, 8), :] += fold(x)


def beside_y(v, low, high):
    rows = v.shape[0]
    row = iota(v.shape, 0)
    below = jnp.where(row == 0, low, pltpu.roll(v, 1, 0))
    above = jnp.where(row == rows - 1, high, pltpu.roll(v, rows - 1, 0))
    return below, above


def beside_z(v):
    return pltpu.roll(v, 1, 1), pltpu.roll(v, v.shape[1] - 1, 1)


def act(i, v, before, after, low, high, faces):
    fx, fyl, fyu, fzl, fzu, diag = faces
    below, above = beside_y(v, low, high)
    left, right = beside_z(v)
    out = diag[i] * v - fx[i] * before - fx[i + 1] * after
    return out - fyl[i] * below - fyu[i] * above - fzl[i] * left - fzu[i] * right


def pack_kernel(ids, x0, coef, z, sx0, sx1, sy0, sy1):
    num, nx, ny, _ = z.shape
    evx, evy = ids[0] == 1, ids[1] == 1
    for f, ref in enumerate([coef, x0] + [z.at[k] for k in range(num)]):
        low, high = ref[0], ref[nx - 1]
        sx0[f], sx1[f] = jnp.where(evx, high, low), jnp.where(evx, low, high)
        low, high = ref[:, 0, :], ref[:, ny - 1, :]
        sy0[f], sy1[f] = jnp.where(evy, high, low), jnp.where(evy, low, high)


def inner_kernel(ids, coef, z, fx, fyl, fyu, fzl, fzu, part, acc):
    num, nx, ny, nz = z.shape
    lane, deep = iota((ny, nz), 1), iota((ny, nz), 0)
    acc[...] = jnp.zeros_like(acc)
    fx[0] = jnp.zeros((ny, nz), F32)
    fx[nx] = jnp.zeros((ny, nz), F32)

    def faces_x(i, carry):
        fx[i] = face(coef[i - 1], coef[i])
        return carry

    lax.fori_loop(1, nx, faces_x, 0)

    def faces_yz(i, carry):
        c = coef[i]
        left, _ = beside_z(c)
        yl = jnp.where(deep == 0, 0.0, face(pltpu.roll(c, 1, 0), c))
        zl = face(jnp.where(lane == 0, 0.0, left), c)
        yu = pltpu.roll(yl, ny - 1, 0)
        zu = jnp.where(lane == nz - 1, c, pltpu.roll(zl, nz - 1, 1))
        fyl[i], fyu[i] = yl, yu
        fzl[i], fzu[i] = jnp.where(lane == 0, 0.0, zl), jnp.where(lane == nz - 1, 0.0, zu)
        part[i] = fx[i + 1] + fx[i] + yu + yl + zu + zl
        return carry

    lax.fori_loop(0, nx, faces_yz, 0, unroll=4)

    def plane(i, carry):
        before, after = jnp.maximum(i - 1, 0), jnp.minimum(i + 1, nx - 1)
        for s in range(0, ny, 8):
            rows = slice(s, s + 8)
            fa, fb, mid = fx[i, rows, :], fx[i + 1, rows, :], part[i, rows, :]
            yl, yu, zl, zu = fyl[i, rows, :], fyu[i, rows, :], fzl[i, rows, :], fzu[i, rows, :]
            strips = [z[k, i, rows, :] for k in range(num)]
            for k, v in enumerate(strips):
                left, right = beside_z(v)
                below = z[k, i, s - 1 : s + 7, :] if s > 0 else pltpu.roll(v, 1, 0)
                above = z[k, i, s + 1 : s + 9, :] if s < ny - 8 else pltpu.roll(v, 7, 0)
                w = mid * v - fa * z[k, before, rows, :] - fb * z[k, after, rows, :]
                w = w - zl * left - zu * right - yl * below - yu * above
                for m in range(k + 1):
                    add_to(acc, m * num + k, w * strips[m])
        return carry

    lax.fori_loop(0, nx, plane, 0, unroll=4)
    for k in range(num):
        for m in range(k):
            acc[pl.ds((k * num + m) * 8, 8), :] = acc[pl.ds((m * num + k) * 8, 8), :]


def prepare_kernel(ids, b, x0, coef, z, rx0, rx1, ry0, ry1, fx_in, fyl_in, fyu_in, fzl, fzu, part, own, fx, fyl, fyu, diag, dinv, r0, zxl, zxh, zyl, zyh, out, xext, yrow, acc, zy0, zy1, row0, row1):
    num, nx, ny, nz = z.shape
    evx, evy = ids[0] == 1, ids[1] == 1
    xext[0] = jnp.where(evx, rx1[1], rx0[1])
    xext[nx + 1] = jnp.where(evx, rx0[1], rx1[1])
    for k in range(num):
        zxl[k] = jnp.where(evx, rx1[2 + k], rx0[2 + k])
        zxh[k] = jnp.where(evx, rx0[2 + k], rx1[2 + k])
        zyl[k] = jnp.where(evy, ry1[2 + k], ry0[2 + k])
        zyh[k] = jnp.where(evy, ry0[2 + k], ry1[2 + k])
        row0[k], row1[k] = z[k, :, 0, :], z[k, :, ny - 1, :]
    for f in range(2):
        yrow[2 * f] = jnp.where(evy, ry1[f], ry0[f])
        yrow[2 * f + 1] = jnp.where(evy, ry0[f], ry1[f])
    square = num * num
    acc[...] = jnp.zeros_like(acc)
    acc[pl.ds(2 * square * 8, square * 8), :] = own[...]
    low_face = face(jnp.where(evx, rx1[0], rx0[0]), coef[0])
    high_face = face(coef[nx - 1], jnp.where(evx, rx0[0], rx1[0]))

    def fill(i, carry):
        xext[i + 1] = x0[i]
        fx[i] = fx_in[i]
        return carry

    lax.fori_loop(0, nx, fill, 0, unroll=4)
    fx[0] = low_face
    fx[nx] = high_face
    low_y = face(yrow[0], coef[:, 0, :])
    high_y = face(coef[:, ny - 1, :], yrow[1])
    for k in range(num):
        zy0[k], zy1[k] = row0[k] * low_y, row1[k] * high_y
    yrow[0] = low_y
    yrow[1] = high_y
    deep = iota((ny, nz), 0)

    def outer(i, carry):
        yl = jnp.where(deep == 0, yrow[0, pl.ds(i, 1), :], fyl_in[i])
        yu = jnp.where(deep == ny - 1, yrow[1, pl.ds(i, 1), :], fyu_in[i])
        d = part[i] + (yl - fyl_in[i]) + (yu - fyu_in[i]) + (fx[i] - fx_in[i]) + (fx[i + 1] - fx_in[i + 1])
        fyl[i], fyu[i] = yl, yu
        diag[i] = d
        dinv[i] = 1.0 / d
        return carry

    lax.fori_loop(0, nx, outer, 0, unroll=4)
    faces = (fx, fyl, fyu, fzl, fzu, diag)

    def plane(i, carry):
        r = b[i] - act(i, xext[i + 1], xext[i], xext[i + 2], yrow[2, pl.ds(i, 1), :], yrow[3, pl.ds(i, 1), :], faces)
        r0[i] = r
        for k in range(num):
            add_to(acc, 3 * square + k, z[k, i] * r)
        return carry

    lax.fori_loop(0, nx, plane, 0, unroll=4)

    def edge_blocks(k, carry):
        low, high = z[k, 0] * fx[0], z[k, nx - 1] * fx[nx]
        for m in range(num):
            add_to(acc, k * num + m, low * zxl[m])
            add_to(acc, square + k * num + m, zy0[k] * zyl[m])
            at = (2 * square + k * num + m) * 8
            acc[pl.ds(at, 8), :] += fold(low * z[m, 0] + high * z[m, nx - 1]) + fold(zy0[k] * row0[m] + zy1[k] * row1[m])
        return carry

    lax.fori_loop(0, num, edge_blocks, 0)
    count = acc.shape[0] // 8
    line = row_of(acc, count, count)
    for piece in range(count // 128):
        out[:, piece, :] = jnp.broadcast_to(line[:, piece * 128 : (piece + 1) * 128], (out.shape[0], 128))


def levels(across):
    found, at, stride = [], 0, 1
    while stride < across:
        count = len(range(stride, across, 2 * stride))
        found.append((at, count, stride))
        at, stride = at + count, 2 * stride
    return found + [(at, 1, 0)]


def column_at(position, across):
    value = jnp.zeros_like(position)
    for at, count, stride in levels(across):
        value = jnp.where((position >= at) & (position < at + count), (position - at) * 2 * stride + stride, value)
    return value


def position_of(column_id, across):
    value = jnp.full_like(column_id, across - 1)
    for at, count, stride in levels(across)[:-1]:
        value = jnp.where(lax.rem(column_id, 2 * stride) == stride, at + lax.div(column_id, 2 * stride), value)
    return value


def device_of(index, num, down, across):
    across_id = column_at(lax.div(index, num * down), across)
    return lax.rem(lax.div(index, num), down) * across + across_id, across_id


def small_inverses(blocks, group=8):
    size = blocks[0].shape[0]
    lane, row, head = iota((size, size), 1), iota((size, size), 0), iota((1, size), 1)
    for start in range(0, size, group):
        wide = [[jnp.broadcast_to(p[:, k : k + 1], (size, size)) for k in range(start, start + group)] for p in blocks]
        for j in range(group):
            k = start + j
            for t, (p, cols) in enumerate(zip(blocks, wide)):
                over = 1.0 / cols[j][k : k + 1, :]
                line = jnp.where(head == k, 1.0, p[k : k + 1, :]) * over
                p = jnp.where(lane == k, 0.0, p) - cols[j] * line
                blocks[t] = jnp.where(row == k, line, p)
                for other in range(j + 1, group):
                    entry = cols[other][k : k + 1, :] * over
                    cols[other] = jnp.where(row == k, entry, cols[other] - cols[j] * entry)
    return blocks


def invert(e, size, across):
    order = e.shape[0]
    for at, count, _ in levels(across):
        low, width = at * size, count * size
        a = e[...]
        parts = small_inverses([a[low + t * size : low + (t + 1) * size, low + t * size : low + (t + 1) * size] for t in range(count)])
        zero = jnp.zeros((size, size), F32)
        pivot = jnp.concatenate([jnp.concatenate([parts[t] if t == u else zero for u in range(count)], 1) for t in range(count)], 0) if count > 1 else parts[0]
        lane = iota((width, order), 1)
        inside = (lane >= low) & (lane < low + width)
        unit = jnp.where(lane == iota((width, order), 0) + low, 1.0, 0.0)
        right = dot(pivot, jnp.where(inside, unit, a[low : low + width, :]))
        row, col = iota((order, order), 0), iota((order, order), 1)
        rest = jnp.where((col >= low) & (col < low + width), 0.0, a) - dot(a[:, low : low + width], right)
        e[...] = rest
        e[low : low + width, :] = right


def column(g, num, order, across, offset, base):
    n = g.shape[0]
    device, _ = device_of(iota((order, n), 0), num, n // across, across)
    pick = jnp.where(iota((order, n), 1) == device + offset, 1.0, 0.0)
    spread = dot(pick, g)
    lane, row = iota(spread.shape, 1), iota(spread.shape, 0)
    return jnp.sum(jnp.where(lane == base + lax.rem(row, num), spread, 0.0), axis=1, keepdims=True)


def matrix_from(got, num, across, e):
    order = e.shape[0]
    n = got.shape[0]
    square = num * num
    down = n // across
    device, _ = device_of(iota((order, n), 0), num, down, across)
    pick = jnp.where(iota((order, n), 1) == device, 1.0, 0.0)
    lane, row = iota((order, 128), 1), iota((order, 128), 0)
    keep = lax.div(lax.rem(lane, square), num) == lax.rem(row, num)
    first = jnp.where(keep, dot(pick, got[:, 0, :]), 0.0)
    second = jnp.where(keep, dot(pick, got[:, 1, :]), 0.0)
    t, c = iota((128, order), 0), iota((128, order), 1)
    same = lax.rem(t, num) == lax.rem(c, num)
    low = jnp.where(same & (t < square), 1.0, 0.0)
    high = jnp.where(same & (t >= square), 1.0, 0.0)
    bi, _ = device_of(iota((order, 1), 0), num, down, across)
    bj, _ = device_of(iota((1, order), 1), num, down, across)
    lower = jnp.where(bj == bi - across, dot(first, low), 0.0) + jnp.where(bj == bi - 1, dot(first, high), 0.0)
    e[...] = jnp.where(bi == bj, dot(second, low), 0.0) - lower - lower.T


def solve(e, col):
    return jnp.sum(e[...] * col, axis=0, keepdims=True)


def amounts(ids, solved, num):
    order = solved.shape[1]
    wide = jnp.broadcast_to(solved, (8, order))
    groups = [pltpu.roll(wide, ids[2 + group], 1) for group in range(5)]
    return [[turned[0:1, k : k + 1] for k in range(num)] for turned in groups]


def combine(y, vectors):
    return functools.reduce(jnp.add, [c * v for c, v in zip(y, vectors)])


def spread_out(ys, z, zxl, zxh, zyl, zyh, gext, gy):
    num, nx, ny, nz = z.shape
    gext[0] = combine(ys[1], [zxl[k] for k in range(num)])
    gext[nx + 1] = combine(ys[2], [zxh[k] for k in range(num)])
    gy[0] = combine(ys[3], [zyl[k] for k in range(num)])
    gy[1] = combine(ys[4], [zyh[k] for k in range(num)])
    wide = [jnp.broadcast_to(c, (ny, nz)) for c in ys[0]]

    def plane(i, carry):
        gext[i + 1] = combine(wide, [z[k, i] for k in range(num)])
        return carry

    lax.fori_loop(0, nx, plane, 0, unroll=4)


def send_rows(i, p, evy, sy0, sy1):
    low, high = p[0:1, :], p[p.shape[0] - 1 :, :]
    sy0[pl.ds(i, 1), :] = jnp.where(evy, high, low)
    sy1[pl.ds(i, 1), :] = jnp.where(evy, low, high)


def send_planes(p, evx, sx0, sx1):
    low, high = p[0], p[p.shape[0] - 1]
    sx0[...] = jnp.where(evx, high, low)
    sx1[...] = jnp.where(evx, low, high)


def start_kernel(across, ids, got, x0, r0, z, zxl, zxh, zyl, zyh, fx, fyl, fyu, fzl, fzu, diag, dinv, e, x, r, p, sx0, sx1, sy0, sy1, gext, gy):
    num, nx, ny, nz = z.shape
    order = e.shape[0]
    matrix_from(got, num, across, e)
    invert(e, got.shape[0] // across * num, across)
    solved = solve(e, column(got[:, 1, :], num, order, across, 0, num * num))
    spread_out(amounts(ids, solved, num), z, zxl, zxh, zyl, zyh, gext, gy)
    faces = (fx, fyl, fyu, fzl, fzu, diag)
    evx, evy = ids[0] == 1, ids[1] == 1

    def plane(i, carry):
        g = gext[i + 1]
        image = act(i, g, gext[i], gext[i + 2], gy[0, pl.ds(i, 1), :], gy[1, pl.ds(i, 1), :], faces)
        x[i] = x0[i] + g
        rest = r0[i] - image
        r[i] = rest
        pre = rest * dinv[i]
        p[i] = pre
        send_rows(i, pre, evy, sy0, sy1)
        return carry

    lax.fori_loop(0, nx, plane, 0, unroll=4)
    send_planes(p, evx, sx0, sx1)


def product_kernel(first, *refs):
    ids, p, r, z, fx, fyl, fyu, fzl, fzu, diag, rx0, rx1, ry0, ry1 = refs[:14]
    applied = None if first else refs[14]
    ap, out, pext, py, acc = refs[-5:]
    num, nx, ny, nz = z.shape
    faces = (fx, fyl, fyu, fzl, fzu, diag)
    evx, evy = ids[0] == 1, ids[1] == 1
    pext[0] = jnp.where(evx, rx1[...], rx0[...])
    pext[nx + 1] = jnp.where(evx, rx0[...], rx1[...])
    py[0] = jnp.where(evy, ry1[...], ry0[...])
    py[1] = jnp.where(evy, ry0[...], ry1[...])
    acc[...] = jnp.zeros_like(acc)

    def fill(i, carry):
        pext[i + 1] = p[i]
        return carry

    lax.fori_loop(0, nx, fill, 0, unroll=4)

    def plane(i, carry):
        v = pext[i + 1]
        w = act(i, v, pext[i], pext[i + 2], py[0, pl.ds(i, 1), :], py[1, pl.ds(i, 1), :], faces)
        ap[i] = w
        add_to(acc, 0, v * r[i])
        add_to(acc, 1, v * w)
        if not first:
            add_to(acc, 2, v * applied[i])
        for k in range(num):
            add_to(acc, 3 + k, w * z[k, i])
        return carry

    lax.fori_loop(0, nx, plane, 0, unroll=4)
    out[:, 0, :] = jnp.broadcast_to(row_of(acc, acc.shape[0] // 8, 128), (out.shape[0], 128))


def update_kernel(first, last, across, *refs):
    ids, got, e, z, zxl, zxh, zyl, zyh, fx, fyl, fyu, fzl, fzu, diag, dinv, p, ap, x, r = refs[:19]
    at = 19
    if not first:
        d_old, ad_old, state_old = refs[at : at + 3]
        at += 3
    d, ad, x_new, r_new, p_new, state = refs[at : at + 6]
    at += 6
    if last:
        out, gext, gy, acc, py = refs[at:]
    else:
        sx0, sx1, sy0, sy1, gext, gy = refs[at:]
    num, nx, ny, nz = z.shape
    order = e.shape[0]
    faces = (fx, fyl, fyu, fzl, fzu, diag)
    g = got[:, 0, :]
    totals = jnp.sum(g, axis=0, keepdims=True)
    new, energy_p, cross = totals[:, 0:1], totals[:, 1:2], totals[:, 2:3]
    col = column(g, num, order, across, 0, 3)
    solved = solve(e, col)
    same = iota((order, order), 0) == iota((order, order), 1)
    line = jnp.sum(jnp.where(same, col, 0.0), axis=0, keepdims=True)
    energy = energy_p - jnp.sum(solved * line, axis=1, keepdims=True)
    if not first:
        beta = new / state_old[0:1, 0:1]
        energy = energy + 2.0 * beta * cross + beta * beta * state_old[1:2, 0:1]
        wide_beta = jnp.broadcast_to(beta, (ny, nz))
    step = jnp.broadcast_to(new / energy, (ny, nz))
    state[0:1, :] = jnp.broadcast_to(new, (1, 128))
    state[1:2, :] = jnp.broadcast_to(energy, (1, 128))
    state[2:8, :] = jnp.zeros((6, 128), F32)
    spread_out(amounts(ids, solved, num), z, zxl, zxh, zyl, zyh, gext, gy)
    evx, evy = ids[0] == 1, ids[1] == 1

    def plane(i, carry):
        c = gext[i + 1]
        image = act(i, c, gext[i], gext[i + 2], gy[0, pl.ds(i, 1), :], gy[1, pl.ds(i, 1), :], faces)
        way, acted = p[i] - c, ap[i] - image
        if not first:
            way, acted = way + wide_beta * d_old[i], acted + wide_beta * ad_old[i]
        d[i] = way
        ad[i] = acted
        x_new[i] = x[i] + step * way
        rest = r[i] - step * acted
        r_new[i] = rest
        pre = rest * dinv[i]
        p_new[i] = pre
        if last:
            add_to(acc, 0, rest * pre)
            py[0, pl.ds(i, 1), :] = pre[0:1, :] * fyl[i, 0:1, :]
            py[1, pl.ds(i, 1), :] = pre[ny - 1 : ny, :] * fyu[i, ny - 1 : ny, :]
        else:
            send_rows(i, pre, evy, sy0, sy1)
        return carry

    if last:
        acc[...] = jnp.zeros_like(acc)
    lax.fori_loop(0, nx, plane, 0, unroll=4)
    if not last:
        send_planes(p_new, evx, sx0, sx1)
        return
    row = iota((ny, nz), 0)

    def second(i, carry):
        v = p_new[i]
        left, right = beside_z(v)
        fa = jnp.where(i > 0, fx[i], 0.0)
        fb = jnp.where(i < nx - 1, fx[i + 1], 0.0)
        w = diag[i] * v - fa * p_new[jnp.maximum(i - 1, 0)] - fb * p_new[jnp.minimum(i + 1, nx - 1)]
        w = w - fzl[i] * left - fzu[i] * right - jnp.where(row == 0, 0.0, fyl[i]) * pltpu.roll(v, 1, 0)
        w = w - jnp.where(row == ny - 1, 0.0, fyu[i]) * pltpu.roll(v, ny - 1, 0)
        for k in range(num):
            add_to(acc, 8 + k, w * z[k, i])
        return carry

    lax.fori_loop(0, nx, second, 0, unroll=4)
    low, high = p_new[0] * fx[0], p_new[nx - 1] * fx[nx]
    for k in range(num):
        add_to(acc, 8 + num + k, -low * zxl[k])
        add_to(acc, 8 + 2 * num + k, -high * zxh[k])
        add_to(acc, 8 + 3 * num + k, -py[0] * zyl[k])
        add_to(acc, 8 + 4 * num + k, -py[1] * zyh[k])
    out[:, 0, :] = jnp.broadcast_to(row_of(acc, acc.shape[0] // 8, 128), (out.shape[0], 128))


def finish_kernel(across, ids, got, e, z, p, d_old, state_old, d):
    num, nx, ny, nz = z.shape
    order = e.shape[0]
    g = got[:, 0, :]
    beta = jnp.sum(g, axis=0, keepdims=True)[:, 0:1] / state_old[0:1, 0:1]
    parts, n = g, g.shape[0]
    for group, offset in ((1, across), (2, -across), (3, 1), (4, -1)):
        moved = pltpu.roll(pltpu.roll(g, (n - offset) % n, 0), 128 - group * num, 1)
        parts = parts + moved
    ys = amounts(ids, solve(e, column(parts, num, order, across, 0, 8)), num)
    wide = [jnp.broadcast_to(c, (ny, nz)) for c in ys[0]]
    wide_beta = jnp.broadcast_to(beta, (ny, nz))

    def plane(i, carry):
        d[i] = p[i] + wide_beta * d_old[i] - combine(wide, [z[k, i] for k in range(num)])
        return carry

    lax.fori_loop(0, nx, plane, 0, unroll=4)


def call(order, kernel, name, args, outs, scratch, cost=None):
    return pl.pallas_call(
        kernel,
        name=name,
        cost_estimate=cost,
        in_specs=[SMEM] + [VMEM] * (len(args) - 1),
        out_specs=[VMEM] * len(outs),
        out_shape=[jax.ShapeDtypeStruct(s, F32) for s in outs],
        scratch_shapes=[pltpu.VMEM(s, F32) for s in scratch],
        compiler_params=pltpu.CompilerParams(vmem_limit_bytes=(16 << 20) + 32 * order * order),
    )(*args)


def per_device(right_side, start_field, coef, deflation):
    num, nx, ny, nz = deflation.shape
    down, across = lax.axis_size("gx"), lax.axis_size("gy")
    n = down * across
    order = n * num
    ix, iy = lax.axis_index("gx"), lax.axis_index("gy")
    evx, evy = ix % 2 == 0, iy % 2 == 0
    shifts = []
    for dx, dy in ((0, 0), (-1, 0), (1, 0), (0, -1), (0, 1)):
        place = position_of(jnp.clip(iy + dy, 0, across - 1), across) * down + jnp.clip(ix + dx, 0, down - 1)
        shifts.append((order - place * num) % order)
    ids = jnp.stack([evx.astype(jnp.int32), evy.astype(jnp.int32)] + shifts)

    field, layer_x, layer_y = (nx, ny, nz), (ny, nz), (nx, nz)
    ext, two_y = (nx + 2, ny, nz), (2, nx, nz)
    layers = [layer_x, layer_x, layer_y, layer_y]
    raw = swaps(
        call(
            order,
            pack_kernel,
            "pack",
            [ids, start_field, coef, deflation],
            [(2 + num,) + layer_x] * 2 + [(2 + num,) + layer_y] * 2,
            [],
        )
    )
    wide = -(-(3 * num * num + num) // 128)
    fx, fyl, fyu, fzl, fzu, part, own = call(
        order,
        inner_kernel,
        "inner",
        [ids, coef, deflation],
        [(nx + 1, ny, nz)] + [field] * 5 + [(num * num * 8, 128)],
        [],
        pl.CostEstimate(flops=250 * num * nx * ny * nz, bytes_accessed=16 << 20, transcendentals=0),
    )
    fx, fyl, fyu, diag, dinv, r0, zxl, zxh, zyl, zyh, out = call(
        order,
        prepare_kernel,
        "prepare",
        [ids, right_side, start_field, coef, deflation, *raw, fx, fyl, fyu, fzl, fzu, part, own],
        [(nx + 1, ny, nz)] + [field] * 5 + [(num,) + layer_x] * 2 + [(num,) + layer_y] * 2 + [(n, wide, 128)],
        [ext, (4, nx, nz), (wide * 128 * 8, 128)] + [(num, nx, nz)] * 4,
    )
    faces = [fx, fyl, fyu, fzl, fzu, diag]
    basis = [deflation, zxl, zxh, zyl, zyh]
    e, x, r, p, *sent = call(
        order,
        functools.partial(start_kernel, across),
        "start",
        [ids, everywhere(out), start_field, r0, *basis, *faces, dinv],
        [(order, order)] + [field] * 3 + layers,
        [ext, two_y],
    )
    old = []
    for iteration in range(ITERS):
        first, last = iteration == 0, iteration == ITERS - 1
        ap, out = call(
            order,
            functools.partial(product_kernel, first),
            "product",
            [ids, p, r, deflation, *faces, *swaps(sent)] + old[1:2],
            [field, (n, 1, 128)],
            [ext, two_y, (16 * 8, 128)],
        )
        d, ad, x, r, p, state, *sent = call(
            order,
            functools.partial(update_kernel, first, last, across),
            "update",
            [ids, everywhere(out), e, *basis, *faces, dinv, p, ap, x, r] + old,
            [field] * 5 + [(8, 128)] + ([(n, 1, 128)] if last else layers),
            [ext, two_y] + ([(48 * 8, 128), two_y] if last else []),
        )
        old = [d, ad, state]
    (direction,) = call(
        order,
        functools.partial(finish_kernel, across),
        "finish",
        [ids, everywhere(sent[0]), e, deflation, p, d, state],
        [field],
        [],
    )
    return x, r, direction


def solution(mesh):
    field = P("gx", "gy", None)
    return jax.shard_map(
        per_device,
        mesh=mesh,
        in_specs=(field, field, field, P(None, "gx", "gy", None)),
        out_specs=(field, field, field),
        check_vma=False,
    )
```

```python
import functools

import jax
import jax.numpy as jnp
from jax import lax
from jax.experimental import pallas as pl
from jax.experimental.pallas import tpu as pltpu
from jax.sharding import PartitionSpec as P

ITERS = 2
BOTH = ("gx", "gy")
HIGH = lax.Precision.HIGHEST
F32 = jnp.float32
VMEM = pl.BlockSpec(memory_space=pltpu.VMEM)
SMEM = pl.BlockSpec(memory_space=pltpu.SMEM)


def swap(value, axis, parity):
    count = lax.axis_size(axis)
    pairs = []
    for low in range(parity, count - 1, 2):
        pairs += [(low, low + 1), (low + 1, low)]
    return lax.ppermute(value, axis, pairs)


def swaps(layers):
    return [swap(v, axis, parity) for v, (axis, parity) in zip(layers, (("gx", 0), ("gx", 1), ("gy", 0), ("gy", 1)))]


def everywhere(payload):
    return lax.all_to_all(payload, BOTH, 0, 0)


def face(lower, upper):
    summed = lower + upper
    inside = (lower > 0.0) & (upper > 0.0)
    return jnp.where(inside, 2.0 * lower * upper / summed, summed)


def iota(shape, dim):
    return lax.broadcasted_iota(jnp.int32, shape, dim)


def dot(a, b):
    return lax.dot_general(a, b, (((1,), (0,)), ((), ())), precision=HIGH, preferred_element_type=F32)


def fold(x):
    pieces = [x[r : r + 8, c : c + 128] for r in range(0, x.shape[0], 8) for c in range(0, x.shape[1], 128)]
    return functools.reduce(jnp.add, pieces)


def row_of(acc, count, width):
    total = functools.reduce(jnp.add, [acc[pl.ds(s, count, stride=8), :] for s in range(8)])
    if width > count:
        total = jnp.concatenate([total, jnp.zeros((width - count, 128), F32)], 0)
    sums = lax.dot_general(jnp.ones((8, 128), F32), total, (((1,), (1,)), ((), ())), precision=HIGH, preferred_element_type=F32)
    return sums[0:1]


def add_to(acc, index, x):
    acc[pl.ds(index * 8, 8), :] += fold(x)


def beside_y(v, low, high):
    rows = v.shape[0]
    row = iota(v.shape, 0)
    below = jnp.where(row == 0, low, pltpu.roll(v, 1, 0))
    above = jnp.where(row == rows - 1, high, pltpu.roll(v, rows - 1, 0))
    return below, above


def beside_z(v):
    return pltpu.roll(v, 1, 1), pltpu.roll(v, v.shape[1] - 1, 1)


def act(i, v, before, after, low, high, faces):
    fx, fyl, fyu, fzl, fzu, diag = faces
    below, above = beside_y(v, low, high)
    left, right = beside_z(v)
    out = diag[i] * v - fx[i] * before - fx[i + 1] * after
    return out - fyl[i] * below - fyu[i] * above - fzl[i] * left - fzu[i] * right


def pack_kernel(ids, two, z, sx0, sx1, sy0, sy1):
    num, nx, ny, _ = z.shape
    evx, evy = ids[0] == 1, ids[1] == 1
    for f, ref in enumerate([two.at[0], two.at[1]] + [z.at[k] for k in range(num)]):
        low, high = ref[0], ref[nx - 1]
        sx0[f], sx1[f] = jnp.where(evx, high, low), jnp.where(evx, low, high)
        low, high = ref[:, 0, :], ref[:, ny - 1, :]
        sy0[f], sy1[f] = jnp.where(evy, high, low), jnp.where(evy, low, high)


def inner_kernel(ids, coef, z, fx, fyl, fyu, fzl, fzu, part, acc):
    num, nx, ny, nz = z.shape
    lane, deep = iota((ny, nz), 1), iota((ny, nz), 0)
    acc[...] = jnp.zeros_like(acc)
    fx[0] = jnp.zeros((ny, nz), F32)
    fx[nx] = jnp.zeros((ny, nz), F32)

    def faces_x(i, carry):
        fx[i] = face(coef[i - 1], coef[i])
        return carry

    lax.fori_loop(1, nx, faces_x, 0)

    def faces_yz(i, carry):
        c = coef[i]
        left, _ = beside_z(c)
        yl = jnp.where(deep == 0, 0.0, face(pltpu.roll(c, 1, 0), c))
        zl = face(jnp.where(lane == 0, 0.0, left), c)
        yu = pltpu.roll(yl, ny - 1, 0)
        zu = jnp.where(lane == nz - 1, c, pltpu.roll(zl, nz - 1, 1))
        fyl[i], fyu[i] = yl, yu
        fzl[i], fzu[i] = jnp.where(lane == 0, 0.0, zl), jnp.where(lane == nz - 1, 0.0, zu)
        part[i] = fx[i + 1] + fx[i] + yu + yl + zu + zl
        return carry

    lax.fori_loop(0, nx, faces_yz, 0, unroll=4)

    def plane(i, carry):
        before, after = jnp.maximum(i - 1, 0), jnp.minimum(i + 1, nx - 1)
        for s in range(0, ny, 8):
            rows = slice(s, s + 8)
            fa, fb, mid = fx[i, rows, :], fx[i + 1, rows, :], part[i, rows, :]
            yl, yu, zl, zu = fyl[i, rows, :], fyu[i, rows, :], fzl[i, rows, :], fzu[i, rows, :]
            strips = [z[k, i, rows, :] for k in range(num)]
            for k, v in enumerate(strips):
                left, right = beside_z(v)
                below = z[k, i, s - 1 : s + 7, :] if s > 0 else pltpu.roll(v, 1, 0)
                above = z[k, i, s + 1 : s + 9, :] if s < ny - 8 else pltpu.roll(v, 7, 0)
                w = mid * v - fa * z[k, before, rows, :] - fb * z[k, after, rows, :]
                w = w - zl * left - zu * right - yl * below - yu * above
                for m in range(k + 1):
                    add_to(acc, m * num + k, w * strips[m])
        return carry

    lax.fori_loop(0, nx, plane, 0, unroll=4)
    for k in range(num):
        for m in range(k):
            acc[pl.ds((k * num + m) * 8, 8), :] = acc[pl.ds((m * num + k) * 8, 8), :]


def prepare_kernel(ids, b, x0, coef, z, rx0, rx1, ry0, ry1, fx_in, fyl_in, fyu_in, fzl, fzu, part, own, fx, fyl, fyu, diag, dinv, r0, zxl, zxh, zyl, zyh, out, xext, yrow, acc, zy0, zy1, row0, row1):
    num, nx, ny, nz = z.shape
    evx, evy = ids[0] == 1, ids[1] == 1
    xext[0] = jnp.where(evx, rx1[1], rx0[1])
    xext[nx + 1] = jnp.where(evx, rx0[1], rx1[1])
    for k in range(num):
        zxl[k] = jnp.where(evx, rx1[2 + k], rx0[2 + k])
        zxh[k] = jnp.where(evx, rx0[2 + k], rx1[2 + k])
        zyl[k] = jnp.where(evy, ry1[2 + k], ry0[2 + k])
        zyh[k] = jnp.where(evy, ry0[2 + k], ry1[2 + k])
        row0[k], row1[k] = z[k, :, 0, :], z[k, :, ny - 1, :]
    for f in range(2):
        yrow[2 * f] = jnp.where(evy, ry1[f], ry0[f])
        yrow[2 * f + 1] = jnp.where(evy, ry0[f], ry1[f])
    square = num * num
    acc[...] = jnp.zeros_like(acc)
    acc[pl.ds(2 * square * 8, square * 8), :] = own[...]
    low_face = face(jnp.where(evx, rx1[0], rx0[0]), coef[0])
    high_face = face(coef[nx - 1], jnp.where(evx, rx0[0], rx1[0]))

    def fill(i, carry):
        xext[i + 1] = x0[i]
        fx[i] = fx_in[i]
        return carry

    lax.fori_loop(0, nx, fill, 0, unroll=4)
    fx[0] = low_face
    fx[nx] = high_face
    low_y = face(yrow[0], coef[:, 0, :])
    high_y = face(coef[:, ny - 1, :], yrow[1])
    for k in range(num):
        zy0[k], zy1[k] = row0[k] * low_y, row1[k] * high_y
    yrow[0] = low_y
    yrow[1] = high_y
    deep = iota((ny, nz), 0)

    def outer(i, carry):
        yl = jnp.where(deep == 0, yrow[0, pl.ds(i, 1), :], fyl_in[i])
        yu = jnp.where(deep == ny - 1, yrow[1, pl.ds(i, 1), :], fyu_in[i])
        d = part[i] + (yl - fyl_in[i]) + (yu - fyu_in[i]) + (fx[i] - fx_in[i]) + (fx[i + 1] - fx_in[i + 1])
        fyl[i], fyu[i] = yl, yu
        diag[i] = d
        dinv[i] = 1.0 / d
        return carry

    lax.fori_loop(0, nx, outer, 0, unroll=4)
    faces = (fx, fyl, fyu, fzl, fzu, diag)

    def plane(i, carry):
        r = b[i] - act(i, xext[i + 1], xext[i], xext[i + 2], yrow[2, pl.ds(i, 1), :], yrow[3, pl.ds(i, 1), :], faces)
        r0[i] = r
        for k in range(num):
            add_to(acc, 3 * square + k, z[k, i] * r)
        return carry

    lax.fori_loop(0, nx, plane, 0, unroll=4)

    def edge_blocks(k, carry):
        low, high = z[k, 0] * fx[0], z[k, nx - 1] * fx[nx]
        for m in range(num):
            add_to(acc, k * num + m, low * zxl[m])
            add_to(acc, square + k * num + m, zy0[k] * zyl[m])
            at = (2 * square + k * num + m) * 8
            acc[pl.ds(at, 8), :] += fold(low * z[m, 0] + high * z[m, nx - 1]) + fold(zy0[k] * row0[m] + zy1[k] * row1[m])
        return carry

    lax.fori_loop(0, num, edge_blocks, 0)
    count = acc.shape[0] // 8
    line = row_of(acc, count, count)
    for piece in range(count // 128):
        out[:, piece, :] = jnp.broadcast_to(line[:, piece * 128 : (piece + 1) * 128], (out.shape[0], 128))


def levels(across):
    found, at, stride = [], 0, 1
    while stride < across:
        count = len(range(stride, across, 2 * stride))
        found.append((at, count, stride))
        at, stride = at + count, 2 * stride
    return found + [(at, 1, 0)]


def column_at(position, across):
    value = jnp.zeros_like(position)
    for at, count, stride in levels(across):
        value = jnp.where((position >= at) & (position < at + count), (position - at) * 2 * stride + stride, value)
    return value


def position_of(column_id, across):
    value = jnp.full_like(column_id, across - 1)
    for at, count, stride in levels(across)[:-1]:
        value = jnp.where(lax.rem(column_id, 2 * stride) == stride, at + lax.div(column_id, 2 * stride), value)
    return value


def device_of(index, num, down, across):
    across_id = column_at(lax.div(index, num * down), across)
    return lax.rem(lax.div(index, num), down) * across + across_id, across_id


def small_inverses(blocks, group=8):
    size = blocks[0].shape[0]
    lane, row, head = iota((size, size), 1), iota((size, size), 0), iota((1, size), 1)
    for start in range(0, size, group):
        wide = [[jnp.broadcast_to(p[:, k : k + 1], (size, size)) for k in range(start, start + group)] for p in blocks]
        for j in range(group):
            k = start + j
            for t, (p, cols) in enumerate(zip(blocks, wide)):
                over = 1.0 / cols[j][k : k + 1, :]
                line = jnp.where(head == k, 1.0, p[k : k + 1, :]) * over
                p = jnp.where(lane == k, 0.0, p) - cols[j] * line
                blocks[t] = jnp.where(row == k, line, p)
                for other in range(j + 1, group):
                    entry = cols[other][k : k + 1, :] * over
                    cols[other] = jnp.where(row == k, entry, cols[other] - cols[j] * entry)
    return blocks


def invert(e, size, across):
    order = e.shape[0]
    for at, count, _ in levels(across):
        low, width = at * size, count * size
        a = e[...]
        parts = small_inverses([a[low + t * size : low + (t + 1) * size, low + t * size : low + (t + 1) * size] for t in range(count)])
        zero = jnp.zeros((size, size), F32)
        pivot = jnp.concatenate([jnp.concatenate([parts[t] if t == u else zero for u in range(count)], 1) for t in range(count)], 0) if count > 1 else parts[0]
        lane = iota((width, order), 1)
        inside = (lane >= low) & (lane < low + width)
        unit = jnp.where(lane == iota((width, order), 0) + low, 1.0, 0.0)
        right = dot(pivot, jnp.where(inside, unit, a[low : low + width, :]))
        row, col = iota((order, order), 0), iota((order, order), 1)
        rest = jnp.where((col >= low) & (col < low + width), 0.0, a) - dot(a[:, low : low + width], right)
        e[...] = rest
        e[low : low + width, :] = right


def column(g, num, order, across, offset, base):
    n = g.shape[0]
    device, _ = device_of(iota((order, n), 0), num, n // across, across)
    pick = jnp.where(iota((order, n), 1) == device + offset, 1.0, 0.0)
    spread = dot(pick, g)
    lane, row = iota(spread.shape, 1), iota(spread.shape, 0)
    return jnp.sum(jnp.where(lane == base + lax.rem(row, num), spread, 0.0), axis=1, keepdims=True)


def matrix_from(got, num, across, e):
    order = e.shape[0]
    n = got.shape[0]
    square = num * num
    down = n // across
    device, _ = device_of(iota((order, n), 0), num, down, across)
    pick = jnp.where(iota((order, n), 1) == device, 1.0, 0.0)
    lane, row = iota((order, 128), 1), iota((order, 128), 0)
    keep = lax.div(lax.rem(lane, square), num) == lax.rem(row, num)
    first = jnp.where(keep, dot(pick, got[:, 0, :]), 0.0)
    second = jnp.where(keep, dot(pick, got[:, 1, :]), 0.0)
    t, c = iota((128, order), 0), iota((128, order), 1)
    same = lax.rem(t, num) == lax.rem(c, num)
    low = jnp.where(same & (t < square), 1.0, 0.0)
    high = jnp.where(same & (t >= square), 1.0, 0.0)
    bi, _ = device_of(iota((order, 1), 0), num, down, across)
    bj, _ = device_of(iota((1, order), 1), num, down, across)
    lower = jnp.where(bj == bi - across, dot(first, low), 0.0) + jnp.where(bj == bi - 1, dot(first, high), 0.0)
    e[...] = jnp.where(bi == bj, dot(second, low), 0.0) - lower - lower.T


def solve(e, col):
    return jnp.sum(e[...] * col, axis=0, keepdims=True)


def amounts(ids, solved, num):
    order = solved.shape[1]
    wide = jnp.broadcast_to(solved, (8, order))
    groups = [pltpu.roll(wide, ids[2 + group], 1) for group in range(5)]
    return [[turned[0:1, k : k + 1] for k in range(num)] for turned in groups]


def combine(y, vectors):
    return functools.reduce(jnp.add, [c * v for c, v in zip(y, vectors)])


def spread_out(ys, z, zxl, zxh, zyl, zyh, gext, gy):
    num, nx, ny, nz = z.shape
    gext[0] = combine(ys[1], [zxl[k] for k in range(num)])
    gext[nx + 1] = combine(ys[2], [zxh[k] for k in range(num)])
    gy[0] = combine(ys[3], [zyl[k] for k in range(num)])
    gy[1] = combine(ys[4], [zyh[k] for k in range(num)])
    wide = [jnp.broadcast_to(c, (ny, nz)) for c in ys[0]]

    def plane(i, carry):
        gext[i + 1] = combine(wide, [z[k, i] for k in range(num)])
        return carry

    lax.fori_loop(0, nx, plane, 0, unroll=4)


def send_rows(i, p, evy, sy0, sy1):
    low, high = p[0:1, :], p[p.shape[0] - 1 :, :]
    sy0[pl.ds(i, 1), :] = jnp.where(evy, high, low)
    sy1[pl.ds(i, 1), :] = jnp.where(evy, low, high)


def send_planes(p, evx, sx0, sx1):
    low, high = p[0], p[p.shape[0] - 1]
    sx0[...] = jnp.where(evx, high, low)
    sx1[...] = jnp.where(evx, low, high)


def start_kernel(across, ids, got, x0, r0, z, zxl, zxh, zyl, zyh, fx, fyl, fyu, fzl, fzu, diag, dinv, e, x, r, p, sx0, sx1, sy0, sy1, gext, gy):
    num, nx, ny, nz = z.shape
    order = e.shape[0]
    matrix_from(got, num, across, e)
    invert(e, got.shape[0] // across * num, across)
    solved = solve(e, column(got[:, 1, :], num, order, across, 0, num * num))
    spread_out(amounts(ids, solved, num), z, zxl, zxh, zyl, zyh, gext, gy)
    faces = (fx, fyl, fyu, fzl, fzu, diag)
    evx, evy = ids[0] == 1, ids[1] == 1

    def plane(i, carry):
        g = gext[i + 1]
        image = act(i, g, gext[i], gext[i + 2], gy[0, pl.ds(i, 1), :], gy[1, pl.ds(i, 1), :], faces)
        x[i] = x0[i] + g
        rest = r0[i] - image
        r[i] = rest
        pre = rest * dinv[i]
        p[i] = pre
        send_rows(i, pre, evy, sy0, sy1)
        return carry

    lax.fori_loop(0, nx, plane, 0, unroll=4)
    send_planes(p, evx, sx0, sx1)


def product_kernel(first, *refs):
    ids, p, r, z, fx, fyl, fyu, fzl, fzu, diag, rx0, rx1, ry0, ry1 = refs[:14]
    applied = None if first else refs[14]
    ap, out, pext, py, acc = refs[-5:]
    num, nx, ny, nz = z.shape
    faces = (fx, fyl, fyu, fzl, fzu, diag)
    evx, evy = ids[0] == 1, ids[1] == 1
    pext[0] = jnp.where(evx, rx1[...], rx0[...])
    pext[nx + 1] = jnp.where(evx, rx0[...], rx1[...])
    py[0] = jnp.where(evy, ry1[...], ry0[...])
    py[1] = jnp.where(evy, ry0[...], ry1[...])
    acc[...] = jnp.zeros_like(acc)

    def fill(i, carry):
        pext[i + 1] = p[i]
        return carry

    lax.fori_loop(0, nx, fill, 0, unroll=4)

    def plane(i, carry):
        v = pext[i + 1]
        w = act(i, v, pext[i], pext[i + 2], py[0, pl.ds(i, 1), :], py[1, pl.ds(i, 1), :], faces)
        ap[i] = w
        add_to(acc, 0, v * r[i])
        add_to(acc, 1, v * w)
        if not first:
            add_to(acc, 2, v * applied[i])
        for k in range(num):
            add_to(acc, 3 + k, w * z[k, i])
        return carry

    lax.fori_loop(0, nx, plane, 0, unroll=4)
    out[:, 0, :] = jnp.broadcast_to(row_of(acc, acc.shape[0] // 8, 128), (out.shape[0], 128))


def update_kernel(first, last, across, *refs):
    ids, got, e, z, zxl, zxh, zyl, zyh, fx, fyl, fyu, fzl, fzu, diag, dinv, p, ap, x, r = refs[:19]
    at = 19
    if not first:
        d_old, ad_old, state_old = refs[at : at + 3]
        at += 3
    d, ad, x_new, r_new, p_new, state = refs[at : at + 6]
    at += 6
    if last:
        out, gext, gy, acc, py = refs[at:]
    else:
        sx0, sx1, sy0, sy1, gext, gy = refs[at:]
    num, nx, ny, nz = z.shape
    order = e.shape[0]
    faces = (fx, fyl, fyu, fzl, fzu, diag)
    g = got[:, 0, :]
    totals = jnp.sum(g, axis=0, keepdims=True)
    new, energy_p, cross = totals[:, 0:1], totals[:, 1:2], totals[:, 2:3]
    col = column(g, num, order, across, 0, 3)
    solved = solve(e, col)
    same = iota((order, order), 0) == iota((order, order), 1)
    line = jnp.sum(jnp.where(same, col, 0.0), axis=0, keepdims=True)
    energy = energy_p - jnp.sum(solved * line, axis=1, keepdims=True)
    if not first:
        beta = new / state_old[0:1, 0:1]
        energy = energy + 2.0 * beta * cross + beta * beta * state_old[1:2, 0:1]
        wide_beta = jnp.broadcast_to(beta, (ny, nz))
    step = jnp.broadcast_to(new / energy, (ny, nz))
    state[0:1, :] = jnp.broadcast_to(new, (1, 128))
    state[1:2, :] = jnp.broadcast_to(energy, (1, 128))
    state[2:8, :] = jnp.zeros((6, 128), F32)
    spread_out(amounts(ids, solved, num), z, zxl, zxh, zyl, zyh, gext, gy)
    evx, evy = ids[0] == 1, ids[1] == 1

    def plane(i, carry):
        c = gext[i + 1]
        image = act(i, c, gext[i], gext[i + 2], gy[0, pl.ds(i, 1), :], gy[1, pl.ds(i, 1), :], faces)
        way, acted = p[i] - c, ap[i] - image
        if not first:
            way, acted = way + wide_beta * d_old[i], acted + wide_beta * ad_old[i]
        d[i] = way
        ad[i] = acted
        x_new[i] = x[i] + step * way
        rest = r[i] - step * acted
        r_new[i] = rest
        pre = rest * dinv[i]
        p_new[i] = pre
        if last:
            add_to(acc, 0, rest * pre)
            py[0, pl.ds(i, 1), :] = pre[0:1, :] * fyl[i, 0:1, :]
            py[1, pl.ds(i, 1), :] = pre[ny - 1 : ny, :] * fyu[i, ny - 1 : ny, :]
        else:
            send_rows(i, pre, evy, sy0, sy1)
        return carry

    if last:
        acc[...] = jnp.zeros_like(acc)
    lax.fori_loop(0, nx, plane, 0, unroll=4)
    if not last:
        send_planes(p_new, evx, sx0, sx1)
        return
    row = iota((ny, nz), 0)

    def second(i, carry):
        v = p_new[i]
        left, right = beside_z(v)
        fa = jnp.where(i > 0, fx[i], 0.0)
        fb = jnp.where(i < nx - 1, fx[i + 1], 0.0)
        w = diag[i] * v - fa * p_new[jnp.maximum(i - 1, 0)] - fb * p_new[jnp.minimum(i + 1, nx - 1)]
        w = w - fzl[i] * left - fzu[i] * right - jnp.where(row == 0, 0.0, fyl[i]) * pltpu.roll(v, 1, 0)
        w = w - jnp.where(row == ny - 1, 0.0, fyu[i]) * pltpu.roll(v, ny - 1, 0)
        for k in range(num):
            add_to(acc, 8 + k, w * z[k, i])
        return carry

    lax.fori_loop(0, nx, second, 0, unroll=4)
    low, high = p_new[0] * fx[0], p_new[nx - 1] * fx[nx]
    for k in range(num):
        add_to(acc, 8 + num + k, -low * zxl[k])
        add_to(acc, 8 + 2 * num + k, -high * zxh[k])
        add_to(acc, 8 + 3 * num + k, -py[0] * zyl[k])
        add_to(acc, 8 + 4 * num + k, -py[1] * zyh[k])
    out[:, 0, :] = jnp.broadcast_to(row_of(acc, acc.shape[0] // 8, 128), (out.shape[0], 128))


def finish_kernel(across, ids, got, e, z, p, d_old, state_old, d):
    num, nx, ny, nz = z.shape
    order = e.shape[0]
    g = got[:, 0, :]
    beta = jnp.sum(g, axis=0, keepdims=True)[:, 0:1] / state_old[0:1, 0:1]
    parts, n = g, g.shape[0]
    for group, offset in ((1, across), (2, -across), (3, 1), (4, -1)):
        moved = pltpu.roll(pltpu.roll(g, (n - offset) % n, 0), 128 - group * num, 1)
        parts = parts + moved
    ys = amounts(ids, solve(e, column(parts, num, order, across, 0, 8)), num)
    wide = [jnp.broadcast_to(c, (ny, nz)) for c in ys[0]]
    wide_beta = jnp.broadcast_to(beta, (ny, nz))

    def plane(i, carry):
        d[i] = p[i] + wide_beta * d_old[i] - combine(wide, [z[k, i] for k in range(num)])
        return carry

    lax.fori_loop(0, nx, plane, 0, unroll=4)


def call(order, kernel, name, args, outs, scratch, cost=None):
    return pl.pallas_call(
        kernel,
        name=name,
        cost_estimate=cost,
        in_specs=[SMEM] + [VMEM] * (len(args) - 1),
        out_specs=[VMEM] * len(outs),
        out_shape=[jax.ShapeDtypeStruct(s, F32) for s in outs],
        scratch_shapes=[pltpu.VMEM(s, F32) for s in scratch],
        compiler_params=pltpu.CompilerParams(vmem_limit_bytes=(16 << 20) + 32 * order * order),
    )(*args)


def per_device(right_side, start_field, coef, deflation):
    num, nx, ny, nz = deflation.shape
    down, across = lax.axis_size("gx"), lax.axis_size("gy")
    n = down * across
    order = n * num
    ix, iy = lax.axis_index("gx"), lax.axis_index("gy")
    evx, evy = ix % 2 == 0, iy % 2 == 0
    shifts = []
    for dx, dy in ((0, 0), (-1, 0), (1, 0), (0, -1), (0, 1)):
        place = position_of(jnp.clip(iy + dy, 0, across - 1), across) * down + jnp.clip(ix + dx, 0, down - 1)
        shifts.append((order - place * num) % order)
    ids = jnp.stack([evx.astype(jnp.int32), evy.astype(jnp.int32)] + shifts)

    field, layer_x, layer_y = (nx, ny, nz), (ny, nz), (nx, nz)
    ext, two_y = (nx + 2, ny, nz), (2, nx, nz)
    layers = [layer_x, layer_x, layer_y, layer_y]
    raw = swaps(
        call(
            order,
            pack_kernel,
            "pack",
            [ids, jnp.stack([coef, start_field]), deflation],
            [(2 + num,) + layer_x] * 2 + [(2 + num,) + layer_y] * 2,
            [],
        )
    )
    wide = -(-(3 * num * num + num) // 128)
    fx, fyl, fyu, fzl, fzu, part, own = call(
        order,
        inner_kernel,
        "inner",
        [ids, coef, deflation],
        [(nx + 1, ny, nz)] + [field] * 5 + [(num * num * 8, 128)],
        [],
        pl.CostEstimate(flops=250 * num * nx * ny * nz, bytes_accessed=16 << 20, transcendentals=0),
    )
    fx, fyl, fyu, diag, dinv, r0, zxl, zxh, zyl, zyh, out = call(
        order,
        prepare_kernel,
        "prepare",
        [ids, right_side, start_field, coef, deflation, *raw, fx, fyl, fyu, fzl, fzu, part, own],
        [(nx + 1, ny, nz)] + [field] * 5 + [(num,) + layer_x] * 2 + [(num,) + layer_y] * 2 + [(n, wide, 128)],
        [ext, (4, nx, nz), (wide * 128 * 8, 128)] + [(num, nx, nz)] * 4,
    )
    faces = [fx, fyl, fyu, fzl, fzu, diag]
    basis = [deflation, zxl, zxh, zyl, zyh]
    e, x, r, p, *sent = call(
        order,
        functools.partial(start_kernel, across),
        "start",
        [ids, everywhere(out), start_field, r0, *basis, *faces, dinv],
        [(order, order)] + [field] * 3 + layers,
        [ext, two_y],
    )
    old = []
    for iteration in range(ITERS):
        first, last = iteration == 0, iteration == ITERS - 1
        ap, out = call(
            order,
            functools.partial(product_kernel, first),
            "product",
            [ids, p, r, deflation, *faces, *swaps(sent)] + old[1:2],
            [field, (n, 1, 128)],
            [ext, two_y, (16 * 8, 128)],
        )
        d, ad, x, r, p, state, *sent = call(
            order,
            functools.partial(update_kernel, first, last, across),
            "update",
            [ids, everywhere(out), e, *basis, *faces, dinv, p, ap, x, r] + old,
            [field] * 5 + [(8, 128)] + ([(n, 1, 128)] if last else layers),
            [ext, two_y] + ([(48 * 8, 128), two_y] if last else []),
        )
        old = [d, ad, state]
    (direction,) = call(
        order,
        functools.partial(finish_kernel, across),
        "finish",
        [ids, everywhere(sent[0]), e, deflation, p, d, state],
        [field],
        [],
    )
    return x, r, direction


def solution(mesh):
    field = P("gx", "gy", None)
    return jax.shard_map(
        per_device,
        mesh=mesh,
        in_specs=(field, field, field, P(None, "gx", "gy", None)),
        out_specs=(field, field, field),
        check_vma=False,
    )
```
